128 devices in a mesh: section: 4 (over y_hi, core), tensor: 8 (over y_lo, z), dp: 4 (over x).
Axes of the slice: x: 4, y: 4 (y_hi: 2, y_lo: 2; y = y_hi * 2 + y_lo), z: 4, core: 2. Of those that a mesh axis runs over, the one named last changes fastest.
Arguments:
- section_inputs: bfloat16 [4, 2, 512, 4096], P('section', None, ('dp', 'tensor')), may hold values from -100 to 100
- gain: float32 [4, 4096], P('section'), may hold values from 0.25 to 1.75
- w_gate: bfloat16 [4, 4096, 5120], P('section', None, 'tensor'), may hold values from -0.09375 to 0.09375
- w_up: bfloat16 [4, 4096, 5120], P('section', None, 'tensor'), may hold values from -0.09375 to 0.09375
- w_down: bfloat16 [4, 5120, 4096], P('section', 'tensor'), may hold values from -0.078125 to 0.078125
- cotangent: bfloat16 [2, 512, 4096], P(None, ('dp', 'tensor')), may hold values from -0.59765625 to 0.59765625
- lengths: int32 [2, 32], P(None, 'dp'), may hold values from 4 to 16, as said below
Outputs:
- grad_gate: bfloat16 [4, 4096, 5120], P('section', 'dp', 'tensor')
- grad_up: bfloat16 [4, 4096, 5120], P('section', 'dp', 'tensor')
- grad_down: bfloat16 [4, 5120, 4096], P('section', 'tensor', 'dp')
- grad_gain: float32 [4, 4096], P('section')
- grad_inputs: bfloat16 [4, 2, 512, 4096], P('section', None, ('dp', 'tensor'))
The draws below stay inside these ranges and needn't reach their ends.
Inputs may be any that keep to these rules, and one draw needn't show every extreme that they name: `lengths`: each sequence's real tokens come first; the rest of its 16 positions are padding. Every micro-batch has a sequence without padding.
All inputs are finite; a program needn't handle non-finite values.
Results may differ from the reference program's by a relative error of at most 0.035.
Values may be sent and summed in bfloat16 or wider, within the bound.
A program may use at most 512 MiB of HBM per device.

```python
import math
import jax
import jax.numpy as jnp
from jax import lax

D = 4096
FF = 5120
LEN = 16
MICRO = 2
SEQS = 8
SECTIONS = 4
BATCH = 32
TOKENS = 512
N_TENSOR = 8
N_DP = 4


def draw_section_inputs(key, part):
    key = jax.random.fold_in(key, 11)
    key_base, key_rows, key_cols = jax.random.split(key, 3)
    shape = (SECTIONS, MICRO, TOKENS, D)
    col_scale = jnp.exp(jax.random.uniform(key_cols, (1, 1, 1, D), jnp.float32, 0.0, math.log(10.0)))
    base = jnp.clip(jax.random.normal(key_base, shape, jnp.float32), -4.0, 4.0)
    row_scale = jnp.exp(jax.random.uniform(key_rows, (SECTIONS, MICRO, TOKENS, 1), jnp.float32, 0.0, math.log(10.0)))
    return (base * row_scale * col_scale / 10.0).astype(jnp.bfloat16)


def draw_lengths(key, part):
    key = jax.random.fold_in(key, 23)
    key_len, key_full = jax.random.split(key)
    drawn = jax.random.randint(key_len, (MICRO, BATCH), LEN // 4, LEN + 1)
    full_seq = jax.random.randint(key_full, (MICRO, 1), 0, BATCH)
    columns = jnp.arange(BATCH, dtype=jnp.int32)[None, :]
    return jnp.where(columns == full_seq, LEN, drawn).astype(jnp.int32)


def level_of(key, shape, cuts, smallest, high):
    loudness = 1.0
    for position, blocks in cuts:
        draws = jax.random.uniform(jax.random.fold_in(jax.random.fold_in(key, 6), position), (blocks,), jnp.float32, smallest / len(cuts), high / len(cuts))
        loudness = loudness * jnp.repeat(jnp.exp(draws), shape[position] // blocks).reshape((-1,) + (1,) * (len(shape) - 1 - position))
    return loudness


def centred(rng, dims, deviation, most, cuts=(), kind=jnp.bfloat16):
    entries = jax.random.normal(rng, dims, jnp.float32) * deviation
    if len(cuts) > 0:
        entries = level_of(rng, dims, cuts, -0.22, 0.18) * entries
    return jnp.clip(entries, min=-most, max=most).astype(kind)


def setup_inputs(seed: int = 0) -> dict:
    seeds = jax.random.split(jax.random.key(seed), 8)
    return {
        "section_inputs": draw_section_inputs(jax.random.fold_in(seeds[7], 71), 0),
        "gain": jnp.clip(1.0 + 0.15 * jax.random.normal(seeds[1], (SECTIONS, D), jnp.float32), 0.25, 1.75),
        "w_gate": centred(seeds[2], (SECTIONS, D, FF), D ** -0.5, 0.09375, ((0, 4), (2, 8))),
        "w_up": centred(seeds[3], (SECTIONS, D, FF), D ** -0.5, 0.09375, ((0, 4), (2, 8))),
        "w_down": centred(seeds[4], (SECTIONS, FF, D), FF ** -0.5, 0.078125, ((0, 4), (1, 8))),
        "cotangent": centred(seeds[5], (MICRO, TOKENS, D), 0.1, 0.59765625, ((1, 32),)),
        "lengths": draw_lengths(jax.random.fold_in(seeds[7], 71), 0),
    }


EPSILON = 1e-06
GELU_SCALE = math.sqrt(2.0 / math.pi)
GELU_CUBIC = 0.044715

def gelu_parts(pre_gate):
    tanh_arg = GELU_SCALE * (pre_gate + GELU_CUBIC * pre_gate * pre_gate * pre_gate)
    tanh_part = jnp.tanh(tanh_arg)
    gelu_value = 0.5 * pre_gate * (1.0 + tanh_part)
    gelu_slope = 0.5 * (1.0 + tanh_part) + 0.5 * pre_gate * (1.0 - tanh_part * tanh_part) * GELU_SCALE * (1.0 + 3.0 * GELU_CUBIC * pre_gate * pre_gate)
    return (gelu_value, gelu_slope)

def rounded(block_term):
    return lax.optimization_barrier(block_term.astype(jnp.bfloat16)).astype(jnp.float32)

def reference(section_inputs, gain, w_gate, w_up, w_down, cotangent, lengths):
    block_width = FF // N_TENSOR
    group_rows = SEQS * LEN
    token_ids = jnp.arange(TOKENS, dtype=jnp.int32)
    positions = token_ids % LEN
    sequences = token_ids // LEN
    incoming = []
    for micro_index in range(MICRO):
        keep_mask = (positions < lengths[micro_index][sequences]).astype(jnp.bfloat16)
        incoming.append(cotangent[micro_index] * keep_mask[:, None])
    grads_gate, grads_up, grads_down, grads_gain, grads_in = ([], [], [], [], [])
    for section_index in reversed(range(SECTIONS)):
        gate_here = w_gate[section_index]
        up_here = w_up[section_index]
        down_here = w_down[section_index]
        gain_here = gain[section_index].astype(jnp.float32)
        saved_rows = []
        outgoing = []
        gain_total = jnp.zeros((D,), jnp.float32)
        for micro_index in range(MICRO):
            rows_float = section_inputs[section_index, micro_index].astype(jnp.float32)
            inv_rms = lax.rsqrt(lax.optimization_barrier(jnp.mean(rows_float * rows_float, axis=-1, keepdims=True)) + EPSILON)
            normed = (rows_float * inv_rms * gain_here).astype(jnp.bfloat16)
            pre_gate = jnp.dot(normed, gate_here, preferred_element_type=jnp.float32)
            pre_up = jnp.dot(normed, up_here, preferred_element_type=jnp.float32)
            gelu_value, gelu_slope = gelu_parts(pre_gate)
            hidden = (gelu_value * pre_up).astype(jnp.bfloat16)
            upstream = incoming[micro_index]
            grad_hidden = jnp.dot(upstream, down_here.T, preferred_element_type=jnp.float32)
            grad_gate_in = (grad_hidden * pre_up * gelu_slope).astype(jnp.bfloat16)
            grad_up_in = (grad_hidden * gelu_value).astype(jnp.bfloat16)
            grad_normed = jnp.zeros((TOKENS, D), jnp.float32)
            for block_index in range(N_TENSOR):
                low_edge = block_index * block_width
                high_edge = low_edge + block_width
                block_term = jnp.dot(grad_gate_in[:, low_edge:high_edge], gate_here[:, low_edge:high_edge].T, preferred_element_type=jnp.float32)
                block_term = block_term + jnp.dot(grad_up_in[:, low_edge:high_edge], up_here[:, low_edge:high_edge].T, preferred_element_type=jnp.float32)
                grad_normed = grad_normed + rounded(block_term)
            scaled = grad_normed * gain_here
            result = upstream.astype(jnp.float32) + inv_rms * scaled - inv_rms * inv_rms * inv_rms * rows_float * lax.optimization_barrier(jnp.mean(scaled * rows_float, axis=-1, keepdims=True))
            outgoing.append(result.astype(jnp.bfloat16))
            gain_total = gain_total + lax.optimization_barrier(jnp.sum(grad_normed * rows_float * inv_rms, axis=0))
            saved_rows.append((normed, hidden, upstream, grad_gate_in, grad_up_in))
        sum_gate = jnp.zeros((D, FF), jnp.float32)
        sum_up = jnp.zeros((D, FF), jnp.float32)
        sum_down = jnp.zeros((FF, D), jnp.float32)
        for group_index in range(N_DP):
            low_edge = group_index * group_rows

            def group_part(member):
                return jnp.concatenate([saved_rows[micro_index][member][low_edge:low_edge + group_rows] for micro_index in range(MICRO)], axis=0)
            normed_rows = group_part(0)
            hidden_rows = group_part(1)
            upstream_rows = group_part(2)
            sum_gate = sum_gate + rounded(jnp.dot(normed_rows.T, group_part(3), preferred_element_type=jnp.float32))
            sum_up = sum_up + rounded(jnp.dot(normed_rows.T, group_part(4), preferred_element_type=jnp.float32))
            sum_down = sum_down + rounded(jnp.dot(hidden_rows.T, upstream_rows, preferred_element_type=jnp.float32))
        grads_gate.append(sum_gate.astype(jnp.bfloat16))
        grads_up.append(sum_up.astype(jnp.bfloat16))
        grads_down.append(sum_down.astype(jnp.bfloat16))
        grads_gain.append(gain_total)
        grads_in.append(jnp.stack(outgoing))
        incoming = outgoing
    return (jnp.stack(grads_gate[::-1]), jnp.stack(grads_up[::-1]), jnp.stack(grads_down[::-1]), jnp.stack(grads_gain[::-1]), jnp.stack(grads_in[::-1]))
```

```python
import functools
import math

import jax
import jax.numpy as jnp
from jax import lax
from jax.experimental import pallas as pl
from jax.experimental.pallas import tpu as pltpu
from jax.sharding import PartitionSpec as P

EPSILON = 1e-06
GELU_SCALE = math.sqrt(2.0 / math.pi)
GELU_CUBIC = 0.044715
MESH = pl.DeviceIdType.MESH
F32 = jnp.float32
BF16 = jnp.bfloat16
MICRO = 2
NN = (((1,), (0,)), ((), ()))
NT = (((1,), (1,)), ((), ()))
TN = (((0,), (0,)), ((), ()))


def dot(a, b, dims):
    return lax.dot_general(a, b, dims, preferred_element_type=F32)


def gelu_parts(pre_gate):
    tanh_arg = GELU_SCALE * (pre_gate + GELU_CUBIC * pre_gate * pre_gate * pre_gate)
    tanh_part = jnp.tanh(tanh_arg)
    gelu_value = 0.5 * pre_gate * (1.0 + tanh_part)
    gelu_slope = 0.5 * (1.0 + tanh_part) + 0.5 * pre_gate * (
        1.0 - tanh_part * tanh_part
    ) * GELU_SCALE * (1.0 + 3.0 * GELU_CUBIC * pre_gate * pre_gate)
    return (gelu_value, gelu_slope)


def kernel(
    dims,
    len_ref, x_ref, gain_ref, cot_ref, wg_hbm, wu_hbm, wd_hbm,
    og_ref, ou_ref, od_ref, ogain_ref, orow_ref,
    w2, wd, nbuf, ubuf, pbuf, rbuf, obuf, nslice, uslice, gall, hall, act, ups, inv_buf,
    gsum, gten, gdp_in, gdp,
    s_w, s_n, r_n, s_u, r_u, s_p, r_p, s_o, r_hop, s_x, r_x, s_gain, r_gain, go,
):
    T, C, R, F, CH = dims
    D = C * CH
    TOK = T * R
    s = lax.axis_index("section")
    t = lax.axis_index("tensor")
    d = lax.axis_index("dp")

    loads = [
        pltpu.make_async_copy(wg_hbm, w2.at[:, pl.ds(0, F)], s_w.at[0]),
        pltpu.make_async_copy(wu_hbm, w2.at[:, pl.ds(F, F)], s_w.at[1]),
        pltpu.make_async_copy(wd_hbm, wd, s_w.at[2]),
    ]
    for load in loads:
        load.start()

    def tpeer(k):
        return lax.rem(t + k, T)

    def dpeer(k):
        return lax.rem(d + k, C)

    barrier = pltpu.get_barrier_semaphore()

    def greet(where):
        pl.semaphore_signal(barrier, inc=1, device_id=where, device_id_type=MESH)

    for k in range(1, T):
        greet({"tensor": tpeer(k)})
    for k in range(1, C):
        greet({"dp": dpeer(k)})
    mate = s + 1 - 2 * lax.rem(s, 2)
    for k in range(T):
        greet({"section": mate, "tensor": lax.rem(t + k, T)})

    @pl.when(s == 1)
    def _():
        greet({"section": 2})

    @pl.when(s == 2)
    def _():
        greet({"section": 1})

    middle = jnp.where((s == 1) | (s == 2), 1, 0)
    pl.semaphore_wait(barrier, (T - 1) + (C - 1) + T + middle)

    def send(src, dst, ssem, rsem, where):
        pltpu.make_async_remote_copy(
            src_ref=src, dst_ref=dst, send_sem=ssem, recv_sem=rsem,
            device_id=where, device_id_type=MESH,
        ).start()

    def wait_for(ref, sem):
        pltpu.make_async_copy(ref, ref, sem).wait()

    def spread(buf, m, c, ssem, rsem):
        for k in range(1, T):
            send(buf.at[m, c, t], buf.at[m, c, t], ssem.at[m, c], rsem.at[m, c], {"tensor": tpeer(k)})

    def others(buf, m, c):
        return buf.at[m, c, pl.ds(0, T - 1)]

    keep_pos = lax.broadcasted_iota(jnp.int32, (R, 1), 0)
    for m in range(MICRO):
        square = jnp.zeros((R, 1), F32)
        for c in range(C):
            part = x_ref[m, :, c * CH : (c + 1) * CH].astype(F32)
            square += jnp.sum(part * part, axis=-1, keepdims=True)
        inv = lax.rsqrt(square * (1.0 / D) + EPSILON)
        inv_buf[m] = jnp.broadcast_to(inv, (R, 128))
        for c in range(C):
            cols = slice(c * CH, (c + 1) * CH)
            part = x_ref[m, :, cols].astype(F32)
            nbuf[m, c, t] = (part * inv * gain_ref[:, cols]).astype(BF16)

    @pl.when(s == 3)
    def _():
        for m in range(MICRO):
            keep = (keep_pos < len_ref[m, t]).astype(F32)
            for c in range(C):
                cols = slice(c * CH, (c + 1) * CH)
                ubuf[m, c, t] = (cot_ref[m, :, cols].astype(F32) * keep).astype(BF16)

    @pl.when(s == 2)
    def _():
        pl.semaphore_wait(go, 1)

    for c in range(C):
        spread(nbuf, 0, c, s_n, r_n)

    @pl.when(s == 3)
    def _():
        for c in range(C):
            spread(ubuf, 0, c, s_u, r_u)

    for load in loads:
        load.wait()

    def exchange_slices(buf, slices, which, m):
        for k in range(1, C):
            j = dpeer(k)
            send(buf.at[m, j], slices.at[m, d], s_x.at[m, which], r_x.at[m, which], {"dp": j})
        slices[m, d] = buf[m, d]

    def exchange_all(buf, which, m):
        for k in range(1, C):
            send(buf.at[m, d], buf.at[m, d], s_x.at[m, which], r_x.at[m, which], {"dp": dpeer(k)})

    def rows_of(buf, m, c):
        return buf[m, c].reshape(TOK, CH)

    def forward(m):
        total = jnp.zeros((TOK, 2 * F), F32)
        for c in range(C):
            total += dot(rows_of(nbuf, m, c), w2[c * CH : (c + 1) * CH, :], NN)
        pre_gate = total[:, :F]
        pre_up = total[:, F:]
        value, slope = gelu_parts(pre_gate)
        act[m] = value
        ups[m] = pre_up * slope
        hall[m, d] = (value * pre_up).astype(BF16)
        exchange_all(hall, 2, m)

    def wait_n(m):
        for c in range(C):
            wait_for(others(nbuf, m, c), r_n.at[m, c])

    wait_n(0)

    @pl.when(s < 3)
    def _():
        for c in range(C):
            spread(nbuf, 1, c, s_n, r_n)
    exchange_slices(nbuf, nslice, 0, 0)
    forward(0)

    @pl.when(s < 3)
    def _():
        wait_n(1)
        exchange_slices(nbuf, nslice, 0, 1)
        forward(1)

    def products(m):
        @pl.when(s == 1)
        def _():
            for c in range(C):
                wait_for(ubuf.at[m, c, t], r_hop.at[m, c])
                spread(ubuf, m, c, s_u, r_u)

        grad_hidden = jnp.zeros((TOK, F), F32)
        for c in range(C):
            @pl.when(lax.rem(s, 2) == 1)
            def _():
                wait_for(others(ubuf, m, c), r_u.at[m, c])

            @pl.when(lax.rem(s, 2) == 0)
            def _():
                wait_for(ubuf.at[m, c], r_u.at[m, c])
            grad_hidden += dot(rows_of(ubuf, m, c), wd[:, c * CH : (c + 1) * CH], NT)
        if m == 0:
            @pl.when(s == 3)
            def _():
                pl.semaphore_signal(go, inc=1, device_id={"section": mate}, device_id_type=MESH)
        gall[m, d, :, :F] = (grad_hidden * ups[m]).astype(BF16)
        gall[m, d, :, F:] = (grad_hidden * act[m]).astype(BF16)
        both = gall[m, d]
        for c in range(C):
            term = dot(both, w2[c * CH : (c + 1) * CH, :], NT).astype(BF16)
            pbuf[m, c] = term.reshape(T, R, CH)
            rbuf[m, c, t] = pbuf[m, c, t]
            for k in range(1, T):
                j = tpeer(k)
                send(pbuf.at[m, c, j], rbuf.at[m, c, t], s_p.at[m, c], r_p.at[m, c], {"tensor": j})
        exchange_all(gall, 3, m)
        exchange_slices(ubuf, uslice, 1, m)

    def finish(m):
        inv = inv_buf[m, :, 0:1]
        mean = jnp.zeros((R, 1), F32)
        sums = []
        for c in range(C):
            cols = slice(c * CH, (c + 1) * CH)
            wait_for(others(rbuf, m, c), r_p.at[m, c])
            grad_normed = jnp.zeros((R, CH), F32)
            for j in range(T):
                grad_normed += rbuf[m, c, j].astype(F32)
            part = x_ref[m, :, cols].astype(F32)
            scaled = grad_normed * gain_ref[:, cols]
            mean += jnp.sum(scaled * part, axis=-1, keepdims=True)
            gain_part = jnp.sum(grad_normed * part * inv, axis=0, keepdims=True)
            if m == 0:
                gsum[:, cols] = gain_part
            else:
                gsum[:, cols] += gain_part
            sums.append(scaled)
        factor = inv * inv * inv * (mean * (1.0 / D))
        for c in range(C):
            cols = slice(c * CH, (c + 1) * CH)
            part = x_ref[m, :, cols].astype(F32)
            result = ubuf[m, c, t].astype(F32) + inv * sums[c] - part * factor
            rows = result.astype(BF16)
            obuf[m, c] = rows
            orow_ref[m, :, cols] = rows

            @pl.when(lax.rem(s, 2) == 1)
            def _():
                for k in range(T):
                    send(obuf.at[m, c], ubuf.at[m, c, t], s_o.at[m, c], r_u.at[m, c],
                         {"section": s - 1, "tensor": lax.rem(t + k, T)})

            @pl.when(s == 2)
            def _():
                send(obuf.at[m, c], ubuf.at[m, c, t], s_o.at[m, c], r_hop.at[m, c], {"section": s - 1})

    products(0)

    @pl.when(s == 3)
    def _():
        for c in range(C):
            spread(nbuf, 1, c, s_n, r_n)
        for c in range(C):
            spread(ubuf, 1, c, s_u, r_u)
        wait_n(1)
        exchange_slices(nbuf, nslice, 0, 1)
        forward(1)

    finish(0)
    products(1)
    finish(1)

    gten[t] = gsum[...]
    for k in range(1, T):
        send(gsum, gten.at[t], s_gain.at[0], r_gain.at[0], {"tensor": tpeer(k)})

    for m in range(MICRO):
        wait_for(nslice.at[m, pl.ds(0, C - 1)], r_x.at[m, 0])
        wait_for(uslice.at[m, pl.ds(0, C - 1)], r_x.at[m, 1])
        wait_for(hall.at[m, pl.ds(0, C - 1)], r_x.at[m, 2])
        wait_for(gall.at[m, pl.ds(0, C - 1)], r_x.at[m, 3])

    count = MICRO * C * TOK
    grads = gall[...].reshape(count, 2 * F)
    step = min(256, CH)
    for n in range(CH // step):
        rows = slice(n * step, (n + 1) * step)
        left = nslice[:, :, :, :, rows].reshape(count, step)
        term = dot(left, grads, TN)
        og_ref[rows, :] = term[:, :F].astype(BF16)
        ou_ref[rows, :] = term[:, F:].astype(BF16)

    wait_for(gten.at[pl.ds(0, T - 1)], r_gain.at[0])
    gain_total = gten[0]
    for j in range(1, T):
        gain_total += gten[j]
    gdp_in[...] = gain_total
    gdp[d] = gain_total
    for k in range(1, C):
        send(gdp_in, gdp.at[d], s_gain.at[1], r_gain.at[1], {"dp": dpeer(k)})

    hidden = hall[...].reshape(count, F)
    for n in range(CH // step):
        cols = slice(n * step, (n + 1) * step)
        right = uslice[:, :, :, :, cols].reshape(count, step)
        od_ref[:, cols] = dot(hidden, right, TN).astype(BF16)

    wait_for(gdp.at[pl.ds(0, C - 1)], r_gain.at[1])
    gain_total = gdp[0]
    for j in range(1, C):
        gain_total += gdp[j]
    ogain_ref[...] = gain_total

    for m in range(MICRO):
        for c in range(C):
            wait_for(others(nbuf, m, c), s_n.at[m, c])
            wait_for(others(pbuf, m, c), s_p.at[m, c])

            @pl.when(lax.rem(s, 2) == 1)
            def _():
                wait_for(others(ubuf, m, c), s_u.at[m, c])
                wait_for(ubuf.at[m, c], s_o.at[m, c])

            @pl.when(s == 2)
            def _():
                wait_for(obuf.at[m, c], s_o.at[m, c])
        wait_for(nslice.at[m, pl.ds(0, C - 1)], s_x.at[m, 0])
        wait_for(uslice.at[m, pl.ds(0, C - 1)], s_x.at[m, 1])
        wait_for(hall.at[m, pl.ds(0, C - 1)], s_x.at[m, 2])
        wait_for(gall.at[m, pl.ds(0, C - 1)], s_x.at[m, 3])
    wait_for(gten.at[pl.ds(0, T - 1)], s_gain.at[0])
    wait_for(gdp.at[pl.ds(0, C - 1)], s_gain.at[1])


def body(T, C, section_inputs, gain, w_gate, w_up, w_down, cotangent, lengths):
    _, micro, R, D = section_inputs.shape
    F = w_gate.shape[2]
    CH = D // C
    TOK = T * R
    dims = (T, C, R, F, CH)
    vmem = pl.BlockSpec(memory_space=pltpu.VMEM)
    smem = pl.BlockSpec(memory_space=pltpu.SMEM)
    hbm = pl.BlockSpec(memory_space=pl.ANY)
    dma = pltpu.SemaphoreType.DMA
    flops = 2 * micro * 8 * TOK * D * F
    outs = pl.pallas_call(
        functools.partial(kernel, dims),
        out_shape=(
            jax.ShapeDtypeStruct((CH, F), BF16),
            jax.ShapeDtypeStruct((CH, F), BF16),
            jax.ShapeDtypeStruct((F, CH), BF16),
            jax.ShapeDtypeStruct((1, D), F32),
            jax.ShapeDtypeStruct((micro, R, D), BF16),
        ),
        in_specs=[smem, vmem, vmem, vmem, hbm, hbm, hbm],
        out_specs=(vmem, vmem, vmem, vmem, vmem),
        scratch_shapes=[
            pltpu.VMEM((D, 2 * F), BF16),
            pltpu.VMEM((F, D), BF16),
            pltpu.VMEM((micro, C, T, R, CH), BF16),
            pltpu.VMEM((micro, C, T, R, CH), BF16),
            pltpu.VMEM((micro, C, T, R, CH), BF16),
            pltpu.VMEM((micro, C, T, R, CH), BF16),
            pltpu.VMEM((micro, C, R, CH), BF16),
            pltpu.VMEM((micro, C, T, R, CH), BF16),
            pltpu.VMEM((micro, C, T, R, CH), BF16),
            pltpu.VMEM((micro, C, TOK, 2 * F), BF16),
            pltpu.VMEM((micro, C, TOK, F), BF16),
            pltpu.VMEM((micro, TOK, F), F32),
            pltpu.VMEM((micro, TOK, F), F32),
            pltpu.VMEM((micro, R, 128), F32),
            pltpu.VMEM((1, D), F32),
            pltpu.VMEM((T, 1, D), F32),
            pltpu.VMEM((1, D), F32),
            pltpu.VMEM((C, 1, D), F32),
            dma((3,)),
            dma((micro, C)),
            dma((micro, C)),
            dma((micro, C)),
            dma((micro, C)),
            dma((micro, C)),
            dma((micro, C)),
            dma((micro, C)),
            dma((micro, C)),
            dma((micro, 4)),
            dma((micro, 4)),
            dma((2,)),
            dma((2,)),
            pltpu.SemaphoreType.REGULAR,
        ],
        cost_estimate=pl.CostEstimate(
            flops=flops, bytes_accessed=24 * D * F // 2, transcendentals=micro * TOK * F
        ),
        compiler_params=pltpu.CompilerParams(
            collective_id=0, has_side_effects=True, vmem_limit_bytes=60 * 1024 * 1024
        ),
    )(lengths, section_inputs[0], gain, cotangent, w_gate[0], w_up[0], w_down[0])
    gate, up, down, gain_out, rows = outs
    return (gate[None], up[None], down[None], gain_out, rows[None])


def solution(mesh):
    T, C = mesh.shape["tensor"], mesh.shape["dp"]
    in_specs = (
        P("section", None, ("dp", "tensor"), None),
        P("section", None),
        P("section", None, "tensor"),
        P("section", None, "tensor"),
        P("section", "tensor", None),
        P(None, ("dp", "tensor"), None),
        P(None, "dp"),
    )
    out_specs = (
        P("section", "dp", "tensor"),
        P("section", "dp", "tensor"),
        P("section", "tensor", "dp"),
        P("section", None),
        P("section", None, ("dp", "tensor"), None),
    )
    return jax.shard_map(
        functools.partial(body, T, C), mesh=mesh, in_specs=in_specs, out_specs=out_specs, check_vma=False
    )
```

```python
import functools
import math

import jax
import jax.numpy as jnp
from jax import lax
from jax.experimental import pallas as pl
from jax.experimental.pallas import tpu as pltpu
from jax.sharding import PartitionSpec as P

EPSILON = 1e-06
GELU_SCALE = math.sqrt(2.0 / math.pi)
GELU_CUBIC = 0.044715
MESH = pl.DeviceIdType.MESH
F32 = jnp.float32
BF16 = jnp.bfloat16
MICRO = 2
NN = (((1,), (0,)), ((), ()))
NT = (((1,), (1,)), ((), ()))
TN = (((0,), (0,)), ((), ()))


def dot(a, b, dims):
    return lax.dot_general(a, b, dims, preferred_element_type=F32)


def gelu_parts(pre_gate):
    tanh_arg = GELU_SCALE * (pre_gate + GELU_CUBIC * pre_gate * pre_gate * pre_gate)
    tanh_part = jnp.tanh(tanh_arg)
    gelu_value = 0.5 * pre_gate * (1.0 + tanh_part)
    gelu_slope = 0.5 * (1.0 + tanh_part) + 0.5 * pre_gate * (
        1.0 - tanh_part * tanh_part
    ) * GELU_SCALE * (1.0 + 3.0 * GELU_CUBIC * pre_gate * pre_gate)
    return (gelu_value, gelu_slope)


def kernel(
    dims,
    len_ref, x_ref, gain_ref, cot_ref, wg_hbm, wu_hbm, wd_hbm,
    og_ref, ou_ref, od_ref, ogain_ref, orow_ref,
    w2, wd, nbuf, ubuf, pbuf, rbuf, obuf, nstage, relay, nslice, uslice, gall, hall, act, ups, inv_buf,
    accg, accd, gsum, gten, gdp_in, gdp,
    s_w, s_n, r_n, s_u, r_u, s_p, r_p, s_o, r_hop, s_l, r_l, s_f, s_x, r_x, s_gain, r_gain, go,
):
    T, C, R, F, CH = dims
    D = C * CH
    TOK = T * R
    HALF = T // 2
    s = lax.axis_index("section")
    t = lax.axis_index("tensor")
    d = lax.axis_index("dp")

    loads = [
        pltpu.make_async_copy(wg_hbm, w2.at[:, pl.ds(0, F)], s_w.at[0]),
        pltpu.make_async_copy(wu_hbm, w2.at[:, pl.ds(F, F)], s_w.at[1]),
        pltpu.make_async_copy(wd_hbm, wd, s_w.at[2]),
    ]
    for load in loads:
        load.start()

    def tpeer(k):
        return lax.rem(t + k, T)

    def dpeer(k):
        return lax.rem(d + k, C)

    barrier = pltpu.get_barrier_semaphore()

    def greet(where):
        pl.semaphore_signal(barrier, inc=1, device_id=where, device_id_type=MESH)

    for k in range(1, T):
        greet({"tensor": tpeer(k)})
    for k in range(1, C):
        greet({"dp": dpeer(k)})
    mate = s + 1 - 2 * lax.rem(s, 2)
    for k in range(T):
        greet({"section": mate, "tensor": lax.rem(t + k, T)})

    @pl.when(s == 1)
    def _():
        greet({"section": 2})

    @pl.when(s == 2)
    def _():
        greet({"section": 1})

    cross = lax.rem(s + 2, 4)
    facing = lax.rem(t + HALF, T)
    odd = lax.rem(s, 2) == 1

    @pl.when(odd)
    def _():
        greet({"section": cross, "tensor": facing})

    @pl.when(jnp.logical_not(odd))
    def _():
        for k in range(T):
            greet({"section": cross, "tensor": lax.rem(t + k, T)})

    middle = jnp.where((s == 1) | (s == 2), 1, 0)

    def send(src, dst, ssem, rsem, where):
        pltpu.make_async_remote_copy(
            src_ref=src, dst_ref=dst, send_sem=ssem, recv_sem=rsem,
            device_id=where, device_id_type=MESH,
        ).start()

    def wait_for(ref, sem):
        pltpu.make_async_copy(ref, ref, sem).wait()

    def spread(buf, m, c, ssem, rsem):
        for k in range(1, T):
            send(buf.at[m, c, t], buf.at[m, c, t], ssem.at[m, c], rsem.at[m, c], {"tensor": tpeer(k)})

    def others(buf, m, c):
        return buf.at[m, c, pl.ds(0, T - 1)]

    keep_pos = lax.broadcasted_iota(jnp.int32, (R, 1), 0)
    for m in range(MICRO):
        square = jnp.zeros((R, 1), F32)
        for c in range(C):
            part = x_ref[m, :, c * CH : (c + 1) * CH].astype(F32)
            square += jnp.sum(part * part, axis=-1, keepdims=True)
        inv = lax.rsqrt(square * (1.0 / D) + EPSILON)
        inv_buf[m] = jnp.broadcast_to(inv, (R, 128))
        for c in range(C):
            cols = slice(c * CH, (c + 1) * CH)
            rows = (x_ref[m, :, cols].astype(F32) * inv * gain_ref[:, cols]).astype(BF16)
            nstage[m, c] = rows

            @pl.when(s != 2)
            def _():
                nbuf[m, c, t] = rows

    def seeds(m, c):
        keep = (keep_pos < len_ref[m, t]).astype(F32)
        return (cot_ref[m, :, c * CH : (c + 1) * CH].astype(F32) * keep).astype(BF16)

    row = (t // HALF) * HALF

    def rowpeer(k):
        return row + lax.rem(t - row + k, HALF)

    def spread_row(buf, m, c, ssem, rsem):
        for k in range(1, HALF):
            send(buf.at[m, c, t], buf.at[m, c, t], ssem.at[m, c], rsem.at[m, c], {"tensor": rowpeer(k)})

    def send_seeds(m):
        for c in range(C):
            spread_row(ubuf, m, c, s_u, r_u)

    @pl.when(s == 3)
    def _():
        for m in range(MICRO):
            for c in range(C):
                ubuf[m, c, t] = seeds(m, c)

    @pl.when(s == 1)
    def _():
        for m in range(MICRO):
            for c in range(C):
                relay[m, c, t] = seeds(m, c)

    pl.semaphore_wait(barrier, (T - 1) + (C - 1) + T + middle + jnp.where(odd, 1, T))
    @pl.when(s == 3)
    def _():
        for c in range(C):
            spread(nbuf, 0, c, s_n, r_n)
        send_seeds(0)

    @pl.when(s == 1)
    def _():
        for m in range(MICRO):
            for c in range(C):
                spread_row(relay, m, c, s_l, r_l)
        for m in range(MICRO):
            for c in range(C):
                wait_for(relay.at[m, c, pl.ds(0, HALF - 1)], r_l.at[m, c])
                part = pl.ds(row, HALF)
                send(relay.at[m, c, part], ubuf.at[m, c, part], s_f.at[m, c], r_u.at[m, c],
                     {"section": cross, "tensor": facing})
            for c in range(C):
                wait_for(relay.at[m, c, pl.ds(0, HALF)], s_f.at[m, c])
            if m == 0:
                pl.semaphore_signal(go, inc=1, device_id={"section": mate}, device_id_type=MESH)

    @pl.when(s == 2)
    def _():
        for m in range(MICRO):
            for c in range(C):
                for k in range(T):
                    send(nstage.at[m, c], relay.at[m, c, t], s_l.at[m, c], r_l.at[m, c],
                         {"section": cross, "tensor": lax.rem(t + k, T)})

    @pl.when(s == 0)
    def _():
        pl.semaphore_wait(go, 1)
        for m in range(MICRO):
            for c in range(C):
                wait_for(relay.at[m, c], r_l.at[m, c])
                send(relay.at[m, c], nbuf.at[m, c], s_f.at[m, c], r_n.at[m, c],
                     {"section": cross, "tensor": facing})
            for c in range(C):
                wait_for(relay.at[m, c], s_f.at[m, c])

    @pl.when(s < 2)
    def _():
        for m in range(MICRO):
            for c in range(C):
                spread(nbuf, m, c, s_n, r_n)

    for load in loads:
        load.wait()

    def exchange_slices(buf, slices, which, m):
        for k in range(1, C):
            j = dpeer(k)
            send(buf.at[m, j], slices.at[m, d], s_x.at[m, which], r_x.at[m, which], {"dp": j})
        slices[m, d] = buf[m, d]

    def exchange_all(buf, which, m):
        for k in range(1, C):
            send(buf.at[m, d], buf.at[m, d], s_x.at[m, which], r_x.at[m, which], {"dp": dpeer(k)})

    def rows_of(buf, m, c):
        return buf[m, c].reshape(TOK, CH)

    def forward(m):
        total = jnp.zeros((TOK, 2 * F), F32)
        for c in range(C):
            total += dot(rows_of(nbuf, m, c), w2[c * CH : (c + 1) * CH, :], NN)
        pre_gate = total[:, :F]
        pre_up = total[:, F:]
        value, slope = gelu_parts(pre_gate)
        act[m] = value
        ups[m] = pre_up * slope
        hall[m, d] = (value * pre_up).astype(BF16)
        exchange_all(hall, 2, m)

    def wait_n(m):
        for c in range(C):
            @pl.when(s == 2)
            def _():
                wait_for(nbuf.at[m, c], r_n.at[m, c])

            @pl.when(s != 2)
            def _():
                wait_for(others(nbuf, m, c), r_n.at[m, c])

    wait_n(0)
    forward(0)
    exchange_slices(nbuf, nslice, 0, 0)

    @pl.when(s < 2)
    def _():
        wait_n(1)
        exchange_slices(nbuf, nslice, 0, 1)
        forward(1)

    def products(m):
        @pl.when(s == 1)
        def _():
            for c in range(C):
                wait_for(ubuf.at[m, c, t], r_hop.at[m, c])
                spread(ubuf, m, c, s_u, r_u)

        grad_hidden = jnp.zeros((TOK, F), F32)
        for c in range(C):
            @pl.when(odd)
            def _():
                wait_for(others(ubuf, m, c), r_u.at[m, c])

            @pl.when(jnp.logical_not(odd))
            def _():
                wait_for(ubuf.at[m, c], r_u.at[m, c])
            grad_hidden += dot(rows_of(ubuf, m, c), wd[:, c * CH : (c + 1) * CH], NT)
        exchange_slices(ubuf, uslice, 1, m)
        gall[m, d, :, :F] = (grad_hidden * ups[m]).astype(BF16)
        gall[m, d, :, F:] = (grad_hidden * act[m]).astype(BF16)
        exchange_all(gall, 3, m)
        both = gall[m, d]
        for c in range(C):
            term = dot(both, w2[c * CH : (c + 1) * CH, :], NT).astype(BF16)
            pbuf[m, c] = term.reshape(T, R, CH)
            rbuf[m, c, t] = pbuf[m, c, t]
            for k in range(1, T):
                j = tpeer(k)
                send(pbuf.at[m, c, j], rbuf.at[m, c, t], s_p.at[m, c], r_p.at[m, c], {"tensor": j})
        if m == 0:
            @pl.when(s == 3)
            def _():
                for c in range(C):
                    spread(nbuf, 1, c, s_n, r_n)
                send_seeds(1)

    def finish(m):
        inv = inv_buf[m, :, 0:1]
        mean = jnp.zeros((R, 1), F32)
        sums = []
        for c in range(C):
            cols = slice(c * CH, (c + 1) * CH)
            wait_for(others(rbuf, m, c), r_p.at[m, c])
            grad_normed = jnp.zeros((R, CH), F32)
            for j in range(T):
                grad_normed += rbuf[m, c, j].astype(F32)
            part = x_ref[m, :, cols].astype(F32)
            scaled = grad_normed * gain_ref[:, cols]
            mean += jnp.sum(scaled * part, axis=-1, keepdims=True)
            gain_part = jnp.sum(grad_normed * part * inv, axis=0, keepdims=True)
            if m == 0:
                gsum[:, cols] = gain_part
            else:
                gsum[:, cols] += gain_part
            sums.append(scaled)
        factor = inv * inv * inv * (mean * (1.0 / D))
        for c in range(C):
            cols = slice(c * CH, (c + 1) * CH)
            part = x_ref[m, :, cols].astype(F32)
            result = ubuf[m, c, t].astype(F32) + inv * sums[c] - part * factor
            rows = result.astype(BF16)
            obuf[m, c] = rows
            orow_ref[m, :, cols] = rows

            @pl.when(odd)
            def _():
                for k in range(T):
                    send(obuf.at[m, c], ubuf.at[m, c, t], s_o.at[m, c], r_u.at[m, c],
                         {"section": s - 1, "tensor": lax.rem(t + k, T)})

            @pl.when(s == 2)
            def _():
                send(obuf.at[m, c], ubuf.at[m, c, t], s_o.at[m, c], r_hop.at[m, c], {"section": s - 1})

    products(0)
    finish(0)

    @pl.when(s >= 2)
    def _():
        wait_n(1)
        forward(1)
        exchange_slices(nbuf, nslice, 0, 1)

    products(1)

    count = C * TOK
    step = min(256, CH)

    def arrived(m):
        wait_for(nslice.at[m, pl.ds(0, C - 1)], r_x.at[m, 0])
        wait_for(uslice.at[m, pl.ds(0, C - 1)], r_x.at[m, 1])
        wait_for(hall.at[m, pl.ds(0, C - 1)], r_x.at[m, 2])
        wait_for(gall.at[m, pl.ds(0, C - 1)], r_x.at[m, 3])

    def term_gate_up(m, rows):
        return dot(nslice[m, :, :, :, rows].reshape(count, step), gall[m].reshape(count, 2 * F), TN)

    def term_down(m, cols):
        return dot(hall[m].reshape(count, F), uslice[m, :, :, :, cols].reshape(count, step), TN)

    def first_terms():
        arrived(0)
        for n in range(CH // step):
            part = slice(n * step, (n + 1) * step)
            accg[part, :] = term_gate_up(0, part)
            accd[:, part] = term_down(0, part)

    pl.when(s == 0)(first_terms)
    finish(1)

    gten[t] = gsum[...]
    for k in range(1, T):
        send(gsum, gten.at[t], s_gain.at[0], r_gain.at[0], {"tensor": tpeer(k)})

    pl.when(s > 0)(first_terms)
    arrived(1)
    for n in range(CH // step):
        rows = slice(n * step, (n + 1) * step)
        total = accg[rows, :] + term_gate_up(1, rows)
        og_ref[rows, :] = total[:, :F].astype(BF16)
        ou_ref[rows, :] = total[:, F:].astype(BF16)

    wait_for(gten.at[pl.ds(0, T - 1)], r_gain.at[0])
    gain_total = gten[0]
    for j in range(1, T):
        gain_total += gten[j]
    gdp_in[...] = gain_total
    gdp[d] = gain_total
    for k in range(1, C):
        send(gdp_in, gdp.at[d], s_gain.at[1], r_gain.at[1], {"dp": dpeer(k)})

    for n in range(CH // step):
        cols = slice(n * step, (n + 1) * step)
        od_ref[:, cols] = (accd[:, cols] + term_down(1, cols)).astype(BF16)

    wait_for(gdp.at[pl.ds(0, C - 1)], r_gain.at[1])
    gain_total = gdp[0]
    for j in range(1, C):
        gain_total += gdp[j]
    ogain_ref[...] = gain_total

    for m in range(MICRO):
        for c in range(C):
            wait_for(others(pbuf, m, c), s_p.at[m, c])

            @pl.when(odd)
            def _():
                wait_for(ubuf.at[m, c], s_o.at[m, c])

            @pl.when(s == 1)
            def _():
                wait_for(relay.at[m, c, pl.ds(0, HALF - 1)], s_l.at[m, c])
                wait_for(others(ubuf, m, c), s_u.at[m, c])

            @pl.when(s == 3)
            def _():
                wait_for(ubuf.at[m, c, pl.ds(0, HALF - 1)], s_u.at[m, c])

            @pl.when(s != 2)
            def _():
                wait_for(others(nbuf, m, c), s_n.at[m, c])

            @pl.when(s == 2)
            def _():
                wait_for(relay.at[m, c], s_l.at[m, c])
                wait_for(obuf.at[m, c], s_o.at[m, c])
        wait_for(nslice.at[m, pl.ds(0, C - 1)], s_x.at[m, 0])
        wait_for(uslice.at[m, pl.ds(0, C - 1)], s_x.at[m, 1])
        wait_for(hall.at[m, pl.ds(0, C - 1)], s_x.at[m, 2])
        wait_for(gall.at[m, pl.ds(0, C - 1)], s_x.at[m, 3])
    wait_for(gten.at[pl.ds(0, T - 1)], s_gain.at[0])
    wait_for(gdp.at[pl.ds(0, C - 1)], s_gain.at[1])


def body(T, C, section_inputs, gain, w_gate, w_up, w_down, cotangent, lengths):
    _, micro, R, D = section_inputs.shape
    F = w_gate.shape[2]
    CH = D // C
    TOK = T * R
    dims = (T, C, R, F, CH)
    vmem = pl.BlockSpec(memory_space=pltpu.VMEM)
    smem = pl.BlockSpec(memory_space=pltpu.SMEM)
    hbm = pl.BlockSpec(memory_space=pl.ANY)
    dma = pltpu.SemaphoreType.DMA
    flops = 2 * micro * 8 * TOK * D * F
    outs = pl.pallas_call(
        functools.partial(kernel, dims),
        out_shape=(
            pltpu.VMEM((CH, F), BF16),
            pltpu.VMEM((CH, F), BF16),
            pltpu.VMEM((F, CH), BF16),
            pltpu.VMEM((1, D), F32),
            pltpu.VMEM((micro, R, D), BF16),
        ),
        in_specs=[smem, vmem, vmem, vmem, hbm, hbm, hbm],
        out_specs=(vmem, vmem, vmem, vmem, vmem),
        scratch_shapes=[
            pltpu.VMEM((D, 2 * F), BF16),
            pltpu.VMEM((F, D), BF16),
            pltpu.VMEM((micro, C, T, R, CH), BF16),
            pltpu.VMEM((micro, C, T, R, CH), BF16),
            pltpu.VMEM((micro, C, T, R, CH), BF16),
            pltpu.VMEM((micro, C, T, R, CH), BF16),
            pltpu.VMEM((micro, C, R, CH), BF16),
            pltpu.VMEM((micro, C, R, CH), BF16),
            pltpu.VMEM((micro, C, T, R, CH), BF16),
            pltpu.VMEM((micro, C, T, R, CH), BF16),
            pltpu.VMEM((micro, C, T, R, CH), BF16),
            pltpu.VMEM((micro, C, TOK, 2 * F), BF16),
            pltpu.VMEM((micro, C, TOK, F), BF16),
            pltpu.VMEM((micro, TOK, F), F32),
            pltpu.VMEM((micro, TOK, F), F32),
            pltpu.VMEM((micro, R, 128), F32),
            pltpu.VMEM((CH, 2 * F), F32),
            pltpu.VMEM((F, CH), F32),
            pltpu.VMEM((1, D), F32),
            pltpu.VMEM((T, 1, D), F32),
            pltpu.VMEM((1, D), F32),
            pltpu.VMEM((C, 1, D), F32),
            dma((3,)),
            dma((micro, C)),
            dma((micro, C)),
            dma((micro, C)),
            dma((micro, C)),
            dma((micro, C)),
            dma((micro, C)),
            dma((micro, C)),
            dma((micro, C)),
            dma((micro, C)),
            dma((micro, C)),
            dma((micro, C)),
            dma((micro, 4)),
            dma((micro, 4)),
            dma((2,)),
            dma((2,)),
            pltpu.SemaphoreType.REGULAR,
        ],
        cost_estimate=pl.CostEstimate(
            flops=flops, bytes_accessed=24 * D * F // 2, transcendentals=micro * TOK * F
        ),
        compiler_params=pltpu.CompilerParams(
            collective_id=0, has_side_effects=True, vmem_limit_bytes=52 * 1024 * 1024
        ),
    )(lengths, section_inputs[0], gain, cotangent, w_gate[0], w_up[0], w_down[0])
    gate, up, down, gain_out, rows = outs
    return (gate[None], up[None], down[None], gain_out, rows[None])


def solution(mesh):
    T, C = mesh.shape["tensor"], mesh.shape["dp"]
    in_specs = (
        P("section", None, ("dp", "tensor"), None),
        P("section", None),
        P("section", None, "tensor"),
        P("section", None, "tensor"),
        P("section", "tensor", None),
        P(None, ("dp", "tensor"), None),
        P(None, "dp"),
    )
    out_specs = (
        P("section", "dp", "tensor"),
        P("section", "dp", "tensor"),
        P("section", "tensor", "dp"),
        P("section", None),
        P("section", None, ("dp", "tensor"), None),
    )
    return jax.shard_map(
        functools.partial(body, T, C), mesh=mesh, in_specs=in_specs, out_specs=out_specs, check_vma=False
    )
```

```python
import functools
import math

import jax
import jax.numpy as jnp
from jax import lax
from jax.experimental import pallas as pl
from jax.experimental.pallas import tpu as pltpu
from jax.sharding import PartitionSpec as P

EPSILON = 1e-06
GELU_SCALE = math.sqrt(2.0 / math.pi)
GELU_CUBIC = 0.044715
MESH = pl.DeviceIdType.MESH
F32 = jnp.float32
BF16 = jnp.bfloat16
MICRO = 2
NN = (((1,), (0,)), ((), ()))
NT = (((1,), (1,)), ((), ()))
TN = (((0,), (0,)), ((), ()))


def dot(a, b, dims):
    return lax.dot_general(a, b, dims, preferred_element_type=F32)


def gelu_parts(pre_gate):
    tanh_arg = GELU_SCALE * (pre_gate + GELU_CUBIC * pre_gate * pre_gate * pre_gate)
    tanh_part = jnp.tanh(tanh_arg)
    gelu_value = 0.5 * pre_gate * (1.0 + tanh_part)
    gelu_slope = 0.5 * (1.0 + tanh_part) + 0.5 * pre_gate * (
        1.0 - tanh_part * tanh_part
    ) * GELU_SCALE * (1.0 + 3.0 * GELU_CUBIC * pre_gate * pre_gate)
    return (gelu_value, gelu_slope)


def kernel(
    dims,
    len_ref, x_ref, gain_ref, cot_ref, wg_hbm, wu_hbm, wd_hbm,
    og_ref, ou_ref, od_ref, ogain_ref, orow_ref,
    w2, wd, nbuf, ubuf, pbuf, rbuf, obuf, nstage, relay, nslice, uslice, pall, hgrad, gall, hall, act, ups, inv_buf,
    accg, accd, gsum, gten, gdp_in, gdp,
    s_w, s_n, r_n, s_u, r_u, s_p, r_p, s_o, r_hop, s_l, r_l, s_f, s_a, r_a, s_x, r_x, s_gain, r_gain, go,
):
    T, C, R, F, CH = dims
    D = C * CH
    TOK = T * R
    HALF = T // 2
    s = lax.axis_index("section")
    t = lax.axis_index("tensor")
    d = lax.axis_index("dp")

    loads = [
        pltpu.make_async_copy(wg_hbm, w2.at[:, pl.ds(0, F)], s_w.at[0]),
        pltpu.make_async_copy(wu_hbm, w2.at[:, pl.ds(F, F)], s_w.at[1]),
        pltpu.make_async_copy(wd_hbm, wd, s_w.at[2]),
    ]
    for load in loads:
        load.start()

    def tpeer(k):
        return lax.rem(t + k, T)

    def dpeer(k):
        return lax.rem(d + k, C)

    barrier = pltpu.get_barrier_semaphore()

    def greet(where):
        pl.semaphore_signal(barrier, inc=1, device_id=where, device_id_type=MESH)

    for k in range(1, T):
        greet({"tensor": tpeer(k)})
    for k in range(1, C):
        greet({"dp": dpeer(k)})
    mate = s + 1 - 2 * lax.rem(s, 2)
    for k in range(T):
        greet({"section": mate, "tensor": lax.rem(t + k, T)})

    @pl.when(s == 1)
    def _():
        greet({"section": 2})

    @pl.when(s == 2)
    def _():
        greet({"section": 1})

    cross = lax.rem(s + 2, 4)
    facing = lax.rem(t + HALF, T)
    odd = lax.rem(s, 2) == 1

    @pl.when(odd)
    def _():
        greet({"section": cross, "tensor": facing})

    @pl.when(jnp.logical_not(odd))
    def _():
        for k in range(T):
            greet({"section": cross, "tensor": lax.rem(t + k, T)})

    middle = jnp.where((s == 1) | (s == 2), 1, 0)

    def send(src, dst, ssem, rsem, where):
        pltpu.make_async_remote_copy(
            src_ref=src, dst_ref=dst, send_sem=ssem, recv_sem=rsem,
            device_id=where, device_id_type=MESH,
        ).start()

    def wait_for(ref, sem):
        pltpu.make_async_copy(ref, ref, sem).wait()

    def spread(buf, m, c, ssem, rsem):
        for k in range(1, T):
            send(buf.at[m, c, t], buf.at[m, c, t], ssem.at[m, c], rsem.at[m, c], {"tensor": tpeer(k)})

    def others(buf, m, c):
        return buf.at[m, c, pl.ds(0, T - 1)]

    keep_pos = lax.broadcasted_iota(jnp.int32, (R, 1), 0)
    for m in range(MICRO):
        square = jnp.zeros((R, 1), F32)
        for c in range(C):
            part = x_ref[m, :, c * CH : (c + 1) * CH].astype(F32)
            square += jnp.sum(part * part, axis=-1, keepdims=True)
        inv = lax.rsqrt(square * (1.0 / D) + EPSILON)
        inv_buf[m] = jnp.broadcast_to(inv, (R, 128))
        for c in range(C):
            cols = slice(c * CH, (c + 1) * CH)
            rows = (x_ref[m, :, cols].astype(F32) * inv * gain_ref[:, cols]).astype(BF16)
            nstage[m, c] = rows

            @pl.when(s != 2)
            def _():
                nbuf[m, c, t] = rows

    def seeds(m, c):
        keep = (keep_pos < len_ref[m, t]).astype(F32)
        return (cot_ref[m, :, c * CH : (c + 1) * CH].astype(F32) * keep).astype(BF16)

    row = (t // HALF) * HALF

    def rowpeer(k):
        return row + lax.rem(t - row + k, HALF)

    def spread_row(buf, m, c, ssem, rsem):
        for k in range(1, HALF):
            send(buf.at[m, c, t], buf.at[m, c, t], ssem.at[m, c], rsem.at[m, c], {"tensor": rowpeer(k)})

    def send_seeds(m):
        for c in range(C):
            spread_row(ubuf, m, c, s_u, r_u)

    @pl.when(s == 3)
    def _():
        for m in range(MICRO):
            for c in range(C):
                ubuf[m, c, t] = seeds(m, c)

    @pl.when(s == 1)
    def _():
        for m in range(MICRO):
            for c in range(C):
                relay[m, c, t] = seeds(m, c)

    pl.semaphore_wait(barrier, (T - 1) + (C - 1) + T + middle + jnp.where(odd, 1, T))
    def spread_n():
        for m in range(MICRO):
            for c in range(C):
                spread(nbuf, m, c, s_n, r_n)

    def slices_over_dp():
        for m in range(MICRO):
            for k in range(1, C):
                j = dpeer(k)
                send(nstage.at[m, j], nslice.at[m, d, t], s_a.at[m], r_a.at[m], {"dp": j})

    def slices_over_tensor():
        for m in range(MICRO):
            wait_for(nslice.at[m, pl.ds(0, C - 1), 0], r_a.at[m])
            for q in range(1, C):
                owner = dpeer(q)
                for k in range(1, T):
                    send(nslice.at[m, owner, t], nslice.at[m, owner, t], s_x.at[m, 0], r_x.at[m, 0],
                         {"tensor": tpeer(k)})

    @pl.when(s == 3)
    def _():
        for m in range(MICRO):
            for c in range(C):
                spread(nbuf, m, c, s_n, r_n)
            send_seeds(m)

    @pl.when(s == 1)
    def _():
        part = pl.ds(row, HALF)
        slices_over_dp()
        for m in range(MICRO):
            for c in range(C):
                spread_row(relay, m, c, s_l, r_l)
        for m in range(MICRO):
            for c in range(C):
                wait_for(relay.at[m, c, pl.ds(0, HALF - 1)], r_l.at[m, c])
                send(relay.at[m, c, part], ubuf.at[m, c, part], s_f.at[m, c], r_u.at[m, c],
                     {"section": cross, "tensor": facing})
        spread_n()
        slices_over_tensor()
        for m in range(MICRO):
            for c in range(C):
                wait_for(relay.at[m, c, pl.ds(0, HALF)], s_f.at[m, c])
        pl.semaphore_signal(go, inc=1, device_id={"section": mate}, device_id_type=MESH)

    @pl.when(s == 2)
    def _():
        for m in range(MICRO):
            for c in range(C):
                for k in range(T):
                    send(nstage.at[m, c], relay.at[m, c, t], s_l.at[m, c], r_l.at[m, c],
                         {"section": cross, "tensor": lax.rem(t + k, T)})

    @pl.when(s == 0)
    def _():
        slices_over_dp()
        for c in range(C):
            wait_for(relay.at[0, c], r_l.at[0, c])
        spread_n()
        slices_over_tensor()
        pl.semaphore_wait(go, 1)
        for m in range(MICRO):
            for c in range(C):
                if m > 0:
                    wait_for(relay.at[m, c], r_l.at[m, c])
                send(relay.at[m, c], nbuf.at[m, c], s_f.at[m, c], r_n.at[m, c],
                     {"section": cross, "tensor": facing})

    for load in loads:
        load.wait()

    def exchange_slices(buf, slices, which, m):
        for k in range(1, C):
            j = dpeer(k)
            send(buf.at[m, j], slices.at[m, d], s_x.at[m, which], r_x.at[m, which], {"dp": j})
        slices[m, d] = buf[m, d]

    def exchange_all(buf, which, m):
        for k in range(1, C):
            send(buf.at[m, d], buf.at[m, d], s_x.at[m, which], r_x.at[m, which], {"dp": dpeer(k)})

    def rows_of(buf, m, c):
        return buf[m, c].reshape(TOK, CH)

    def forward(m):
        total = jnp.zeros((TOK, 2 * F), F32)
        for c in range(C):
            @pl.when(s == 2)
            def _():
                wait_for(nbuf.at[m, c], r_n.at[m, c])

            @pl.when(s != 2)
            def _():
                wait_for(others(nbuf, m, c), r_n.at[m, c])
            total += dot(rows_of(nbuf, m, c), w2[c * CH : (c + 1) * CH, :], NN)
        pall[m, d] = total.astype(BF16)
        exchange_all(pall, 2, m)
        pre_up = total[:, F:]
        value, slope = gelu_parts(total[:, :F])
        act[m] = value
        ups[m] = pre_up * slope

        @pl.when(s >= 2)
        def _():
            exchange_slices(nbuf, nslice, 0, m)

        @pl.when(s < 2)
        def _():
            nslice[m, d] = nbuf[m, d]

    def expand(m):
        wait_for(pall.at[m, pl.ds(0, C - 1)], r_x.at[m, 2])
        wait_for(pall.at[m, pl.ds(0, C - 1)], s_x.at[m, 2])

        def one(j, carry):
            pre_gate = pall[m, j, :, :F].astype(F32)
            pre_up = pall[m, j, :, F:].astype(F32)
            value, slope = gelu_parts(pre_gate)
            hall[m, j] = (value * pre_up).astype(BF16)
            pall[m, j, :, :F] = (pre_up * slope).astype(BF16)
            pall[m, j, :, F:] = value.astype(BF16)
            return carry

        lax.fori_loop(0, C, one, 0)

    def expand_grads(m):
        def one(j, carry):
            upstream = hgrad[m, j].astype(F32)
            gall[m, j, :, :F] = (upstream * pall[m, j, :, :F].astype(F32)).astype(BF16)
            gall[m, j, :, F:] = (upstream * pall[m, j, :, F:].astype(F32)).astype(BF16)
            return carry

        lax.fori_loop(0, C, one, 0)

    def products(m):
        grad_hidden = jnp.zeros((TOK, F), F32)
        for c in range(C):
            @pl.when(odd)
            def _():
                wait_for(others(ubuf, m, c), r_u.at[m, c])

            @pl.when(jnp.logical_not(odd))
            def _():
                wait_for(ubuf.at[m, c], r_u.at[m, c])
            grad_hidden += dot(rows_of(ubuf, m, c), wd[:, c * CH : (c + 1) * CH], NT)
        exchange_slices(ubuf, uslice, 1, m)
        hgrad[m, d] = grad_hidden.astype(BF16)
        exchange_all(hgrad, 3, m)
        both = jnp.concatenate(
            [(grad_hidden * ups[m]).astype(BF16), (grad_hidden * act[m]).astype(BF16)], axis=1
        )
        for c in range(C):
            term = dot(both, w2[c * CH : (c + 1) * CH, :], NT).astype(BF16)
            pbuf[m, c] = term.reshape(T, R, CH)
            rbuf[m, c, t] = pbuf[m, c, t]
            for k in range(1, T):
                j = tpeer(k)
                send(pbuf.at[m, c, j], rbuf.at[m, c, t], s_p.at[m, c], r_p.at[m, c], {"tensor": j})
    def finish(m):
        inv = inv_buf[m, :, 0:1]
        mean = jnp.zeros((R, 1), F32)
        sums = []
        for c in range(C):
            cols = slice(c * CH, (c + 1) * CH)
            wait_for(others(rbuf, m, c), r_p.at[m, c])
            grad_normed = jnp.zeros((R, CH), F32)
            for j in range(T):
                grad_normed += rbuf[m, c, j].astype(F32)
            part = x_ref[m, :, cols].astype(F32)
            scaled = grad_normed * gain_ref[:, cols]
            mean += jnp.sum(scaled * part, axis=-1, keepdims=True)
            gain_part = jnp.sum(grad_normed * part * inv, axis=0, keepdims=True)
            if m == 0:
                gsum[:, cols] = gain_part
            else:
                gsum[:, cols] += gain_part
            sums.append(scaled)
        factor = inv * inv * inv * (mean * (1.0 / D))
        for c in range(C):
            cols = slice(c * CH, (c + 1) * CH)
            part = x_ref[m, :, cols].astype(F32)
            result = ubuf[m, c, t].astype(F32) + inv * sums[c] - part * factor
            rows = result.astype(BF16)
            obuf[m, c] = rows
            orow_ref[m, :, cols] = rows

            @pl.when(odd)
            def _():
                for k in range(T):
                    send(obuf.at[m, c], ubuf.at[m, c, t], s_o.at[m, c], r_u.at[m, c],
                         {"section": s - 1, "tensor": lax.rem(t + k, T)})

            @pl.when(s == 2)
            def _():
                send(obuf.at[m, c], ubuf.at[m, c, t], s_o.at[m, c], r_hop.at[m, c], {"section": s - 1})

    forward(0)
    pl.when(s < 2)(lambda: forward(1))

    @pl.when(s == 1)
    def _():
        for m in range(MICRO):
            for c in range(C):
                wait_for(ubuf.at[m, c, t], r_hop.at[m, c])
                spread(ubuf, m, c, s_u, r_u)

    products(0)
    pl.when(s >= 2)(lambda: forward(1))
    products(1)

    @pl.when(s == 0)
    def _():
        for m in range(MICRO):
            expand(m)

    finish(0)

    count = C * TOK
    step = min(256, CH)

    def arrived(m):
        @pl.when(s >= 2)
        def _():
            wait_for(nslice.at[m, pl.ds(0, C - 1)], r_x.at[m, 0])

        @pl.when(s < 2)
        def _():
            wait_for(nslice.at[m, pl.ds(0, C - 1), pl.ds(0, T - 1)], r_x.at[m, 0])

        wait_for(uslice.at[m, pl.ds(0, C - 1)], r_x.at[m, 1])
        wait_for(hgrad.at[m, pl.ds(0, C - 1)], r_x.at[m, 3])
        expand_grads(m)

    def term_gate_up(m, rows):
        return dot(nslice[m, :, :, :, rows].reshape(count, step), gall[m].reshape(count, 2 * F), TN)

    def term_down(m, cols):
        return dot(hall[m].reshape(count, F), uslice[m, :, :, :, cols].reshape(count, step), TN)

    def first_terms():
        arrived(0)
        for n in range(CH // step):
            part = slice(n * step, (n + 1) * step)
            accg[part, :] = term_gate_up(0, part)
            accd[:, part] = term_down(0, part)

    pl.when(s == 0)(first_terms)
    finish(1)

    gten[t] = gsum[...]
    for k in range(1, T):
        send(gsum, gten.at[t], s_gain.at[0], r_gain.at[0], {"tensor": tpeer(k)})

    @pl.when(s > 0)
    def _():
        for m in range(MICRO):
            expand(m)
        first_terms()

    arrived(1)
    for n in range(CH // step):
        rows = slice(n * step, (n + 1) * step)
        total = accg[rows, :] + term_gate_up(1, rows)
        og_ref[rows, :] = total[:, :F].astype(BF16)
        ou_ref[rows, :] = total[:, F:].astype(BF16)

    wait_for(gten.at[pl.ds(0, T - 1)], r_gain.at[0])
    gain_total = gten[0]
    for j in range(1, T):
        gain_total += gten[j]
    gdp_in[...] = gain_total
    gdp[d] = gain_total
    for k in range(1, C):
        send(gdp_in, gdp.at[d], s_gain.at[1], r_gain.at[1], {"dp": dpeer(k)})

    for n in range(CH // step):
        cols = slice(n * step, (n + 1) * step)
        od_ref[:, cols] = (accd[:, cols] + term_down(1, cols)).astype(BF16)

    wait_for(gdp.at[pl.ds(0, C - 1)], r_gain.at[1])
    gain_total = gdp[0]
    for j in range(1, C):
        gain_total += gdp[j]
    ogain_ref[...] = gain_total

    for m in range(MICRO):
        for c in range(C):
            wait_for(others(pbuf, m, c), s_p.at[m, c])

            @pl.when(odd)
            def _():
                wait_for(ubuf.at[m, c], s_o.at[m, c])

            @pl.when(s == 0)
            def _():
                wait_for(relay.at[m, c], s_f.at[m, c])

            @pl.when(s == 1)
            def _():
                wait_for(relay.at[m, c, pl.ds(0, HALF - 1)], s_l.at[m, c])
                wait_for(others(ubuf, m, c), s_u.at[m, c])

            @pl.when(s == 3)
            def _():
                wait_for(ubuf.at[m, c, pl.ds(0, HALF - 1)], s_u.at[m, c])

            @pl.when(s != 2)
            def _():
                wait_for(others(nbuf, m, c), s_n.at[m, c])

            @pl.when(s == 2)
            def _():
                wait_for(relay.at[m, c], s_l.at[m, c])
                wait_for(obuf.at[m, c], s_o.at[m, c])
        @pl.when(s >= 2)
        def _():
            wait_for(nslice.at[m, pl.ds(0, C - 1)], s_x.at[m, 0])

        @pl.when(s < 2)
        def _():
            wait_for(nslice.at[m, pl.ds(0, C - 1), 0], s_a.at[m])
            wait_for(nslice.at[m, pl.ds(0, C - 1), pl.ds(0, T - 1)], s_x.at[m, 0])

        wait_for(uslice.at[m, pl.ds(0, C - 1)], s_x.at[m, 1])
        wait_for(hgrad.at[m, pl.ds(0, C - 1)], s_x.at[m, 3])
    wait_for(gten.at[pl.ds(0, T - 1)], s_gain.at[0])
    wait_for(gdp.at[pl.ds(0, C - 1)], s_gain.at[1])


def writer(*refs):
    count = len(refs) // 2
    sems = refs[-1]
    copies = [pltpu.make_async_copy(refs[i], refs[count + i], sems.at[i]) for i in range(count)]
    for copy in copies:
        copy.start()
    for copy in copies:
        copy.wait()


def body(T, C, section_inputs, gain, w_gate, w_up, w_down, cotangent, lengths):
    _, micro, R, D = section_inputs.shape
    F = w_gate.shape[2]
    CH = D // C
    TOK = T * R
    dims = (T, C, R, F, CH)
    vmem = pl.BlockSpec(memory_space=pltpu.VMEM)
    smem = pl.BlockSpec(memory_space=pltpu.SMEM)
    hbm = pl.BlockSpec(memory_space=pl.ANY)
    dma = pltpu.SemaphoreType.DMA
    flops = 2 * micro * 8 * TOK * D * F
    outs = pl.pallas_call(
        functools.partial(kernel, dims),
        out_shape=(
            pltpu.VMEM((CH, F), BF16),
            pltpu.VMEM((CH, F), BF16),
            pltpu.VMEM((F, CH), BF16),
            pltpu.VMEM((1, D), F32),
            pltpu.VMEM((micro, R, D), BF16),
        ),
        in_specs=[smem, vmem, vmem, vmem, hbm, hbm, hbm],
        out_specs=(vmem, vmem, vmem, vmem, vmem),
        scratch_shapes=[
            pltpu.VMEM((D, 2 * F), BF16),
            pltpu.VMEM((F, D), BF16),
            pltpu.VMEM((micro, C, T, R, CH), BF16),
            pltpu.VMEM((micro, C, T, R, CH), BF16),
            pltpu.VMEM((micro, C, T, R, CH), BF16),
            pltpu.VMEM((micro, C, T, R, CH), BF16),
            pltpu.VMEM((micro, C, R, CH), BF16),
            pltpu.VMEM((micro, C, R, CH), BF16),
            pltpu.VMEM((micro, C, T, R, CH), BF16),
            pltpu.VMEM((micro, C, T, R, CH), BF16),
            pltpu.VMEM((micro, C, T, R, CH), BF16),
            pltpu.VMEM((micro, C, TOK, 2 * F), BF16),
            pltpu.VMEM((micro, C, TOK, F), BF16),
            pltpu.VMEM((micro, C, TOK, 2 * F), BF16),
            pltpu.VMEM((micro, C, TOK, F), BF16),
            pltpu.VMEM((micro, TOK, F), F32),
            pltpu.VMEM((micro, TOK, F), F32),
            pltpu.VMEM((micro, R, 128), F32),
            pltpu.VMEM((CH, 2 * F), F32),
            pltpu.VMEM((F, CH), F32),
            pltpu.VMEM((1, D), F32),
            pltpu.VMEM((T, 1, D), F32),
            pltpu.VMEM((1, D), F32),
            pltpu.VMEM((C, 1, D), F32),
            dma((3,)),
            dma((micro, C)),
            dma((micro, C)),
            dma((micro, C)),
            dma((micro, C)),
            dma((micro, C)),
            dma((micro, C)),
            dma((micro, C)),
            dma((micro, C)),
            dma((micro, C)),
            dma((micro, C)),
            dma((micro, C)),
            dma((micro,)),
            dma((micro,)),
            dma((micro, 4)),
            dma((micro, 4)),
            dma((2,)),
            dma((2,)),
            pltpu.SemaphoreType.REGULAR,
        ],
        cost_estimate=pl.CostEstimate(
            flops=flops, bytes_accessed=24 * D * F // 2, transcendentals=micro * TOK * F
        ),
        compiler_params=pltpu.CompilerParams(
            collective_id=0, has_side_effects=True, vmem_limit_bytes=54 * 1024 * 1024
        ),
    )(lengths, section_inputs[0], gain, cotangent, w_gate[0], w_up[0], w_down[0])
    gate, up, down, gain_out, rows = pl.pallas_call(
        writer,
        out_shape=tuple(jax.ShapeDtypeStruct(out.shape, out.dtype) for out in outs),
        in_specs=[vmem] * len(outs),
        out_specs=(hbm,) * len(outs),
        scratch_shapes=[dma((len(outs),))],
    )(*outs)
    return (gate[None], up[None], down[None], gain_out, rows[None])


def solution(mesh):
    T, C = mesh.shape["tensor"], mesh.shape["dp"]
    in_specs = (
        P("section", None, ("dp", "tensor"), None),
        P("section", None),
        P("section", None, "tensor"),
        P("section", None, "tensor"),
        P("section", "tensor", None),
        P(None, ("dp", "tensor"), None),
        P(None, "dp"),
    )
    out_specs = (
        P("section", "dp", "tensor"),
        P("section", "dp", "tensor"),
        P("section", "tensor", "dp"),
        P("section", None),
        P("section", None, ("dp", "tensor"), None),
    )
    return jax.shard_map(
        functools.partial(body, T, C), mesh=mesh, in_specs=in_specs, out_specs=out_specs, check_vma=False
    )
```

```python
import functools
import math

import jax
import jax.numpy as jnp
from jax import lax
from jax.experimental import pallas as pl
from jax.experimental.pallas import tpu as pltpu
from jax.sharding import PartitionSpec as P

EPSILON = 1e-06
GELU_SCALE = math.sqrt(2.0 / math.pi)
GELU_CUBIC = 0.044715
MESH = pl.DeviceIdType.MESH
F32 = jnp.float32
BF16 = jnp.bfloat16
MICRO = 2
NN = (((1,), (0,)), ((), ()))
NT = (((1,), (1,)), ((), ()))
TN = (((0,), (0,)), ((), ()))


def dot(a, b, dims):
    return lax.dot_general(a, b, dims, preferred_element_type=F32)


def gelu_parts(pre_gate):
    tanh_arg = GELU_SCALE * (pre_gate + GELU_CUBIC * pre_gate * pre_gate * pre_gate)
    tanh_part = jnp.tanh(tanh_arg)
    gelu_value = 0.5 * pre_gate * (1.0 + tanh_part)
    gelu_slope = 0.5 * (1.0 + tanh_part) + 0.5 * pre_gate * (
        1.0 - tanh_part * tanh_part
    ) * GELU_SCALE * (1.0 + 3.0 * GELU_CUBIC * pre_gate * pre_gate)
    return (gelu_value, gelu_slope)


def kernel(
    dims,
    len_ref, x_hbm, gain_hbm, cot_hbm, wg_hbm, wu_hbm, wd_hbm,
    od_ref, ogain_ref, orow_ref, accg, nslice, gall,
    x_ref, gain_ref, cot_ref, w2, wd, wdt, nbuf, ubuf, pbuf, rbuf, obuf, nstage, relay, uslice, pall, hgrad, hall, act, ups, inv_buf,
    accd, gsum, gten, gdp_in, gdp,
    s_w, s_d, s_n, r_n, s_u, r_u, s_p, r_p, s_o, r_hop, s_l, r_l, s_f, s_a, r_a, s_x, r_x, s_gain, r_gain, go,
):
    T, C, R, F, CH = dims
    D = C * CH
    TOK = T * R
    HALF = T // 2
    s = lax.axis_index("section")
    t = lax.axis_index("tensor")
    d = lax.axis_index("dp")

    def tpeer(k):
        return lax.rem(t + k, T)

    def dpeer(k):
        return lax.rem(d + k, C)

    barrier = pltpu.get_barrier_semaphore()

    def greet(where):
        pl.semaphore_signal(barrier, inc=1, device_id=where, device_id_type=MESH)

    for k in range(1, T):
        greet({"tensor": tpeer(k)})
    for k in range(1, C):
        greet({"dp": dpeer(k)})
    mate = s + 1 - 2 * lax.rem(s, 2)
    for k in range(T):
        greet({"section": mate, "tensor": lax.rem(t + k, T)})

    @pl.when(s == 1)
    def _():
        greet({"section": 2})

    @pl.when(s == 2)
    def _():
        greet({"section": 1})

    cross = lax.rem(s + 2, 4)
    facing = lax.rem(t + HALF, T)
    odd = lax.rem(s, 2) == 1

    @pl.when(odd)
    def _():
        greet({"section": cross, "tensor": facing})

    @pl.when(jnp.logical_not(odd))
    def _():
        for k in range(T):
            greet({"section": cross, "tensor": lax.rem(t + k, T)})

    middle = jnp.where((s == 1) | (s == 2), 1, 0)

    def send(src, dst, ssem, rsem, where):
        pltpu.make_async_remote_copy(
            src_ref=src, dst_ref=dst, send_sem=ssem, recv_sem=rsem,
            device_id=where, device_id_type=MESH,
        ).start()

    def wait_for(ref, sem):
        pltpu.make_async_copy(ref, ref, sem).wait()

    def spread(buf, m, c, ssem, rsem):
        for k in range(1, T):
            send(buf.at[m, c, t], buf.at[m, c, t], ssem.at[m, c], rsem.at[m, c], {"tensor": tpeer(k)})

    def others(buf, m, c):
        return buf.at[m, c, pl.ds(0, T - 1)]

    inputs = [
        pltpu.make_async_copy(x_hbm, x_ref, s_w.at[3]),
        pltpu.make_async_copy(gain_hbm, gain_ref, s_w.at[4]),
        pltpu.make_async_copy(cot_hbm, cot_ref, s_w.at[5]),
    ]
    for load in inputs:
        load.start()
    loads = [
        pltpu.make_async_copy(wg_hbm, w2.at[:, pl.ds(0, F)], s_w.at[0]),
        pltpu.make_async_copy(wu_hbm, w2.at[:, pl.ds(F, F)], s_w.at[1]),
    ]
    for load in loads:
        load.start()
    for c in range(min(2, C)):
        pltpu.make_async_copy(wd_hbm.at[:, pl.ds(c * CH, CH)], wd.at[c], s_d.at[c]).start()

    for load in inputs:
        load.wait()

    keep_pos = lax.broadcasted_iota(jnp.int32, (R, 1), 0)
    for m in range(MICRO):
        square = jnp.zeros((R, 1), F32)
        for c in range(C):
            part = x_ref[m, :, c * CH : (c + 1) * CH].astype(F32)
            square += jnp.sum(part * part, axis=-1, keepdims=True)
        inv = lax.rsqrt(square * (1.0 / D) + EPSILON)
        inv_buf[m] = jnp.broadcast_to(inv, (R, 128))
        for c in range(C):
            cols = slice(c * CH, (c + 1) * CH)
            rows = (x_ref[m, :, cols].astype(F32) * inv * gain_ref[:, cols]).astype(BF16)
            nstage[m, c] = rows

            @pl.when(s != 2)
            def _():
                nbuf[m, c, t] = rows

    def seeds(m, c):
        keep = (keep_pos < len_ref[m, t]).astype(F32)
        return (cot_ref[m, :, c * CH : (c + 1) * CH].astype(F32) * keep).astype(BF16)

    row = (t // HALF) * HALF

    def rowpeer(k):
        return row + lax.rem(t - row + k, HALF)

    def spread_row(buf, m, c, ssem, rsem):
        for k in range(1, HALF):
            send(buf.at[m, c, t], buf.at[m, c, t], ssem.at[m, c], rsem.at[m, c], {"tensor": rowpeer(k)})

    def send_seeds(m):
        for c in range(C):
            spread_row(ubuf, m, c, s_u, r_u)

    @pl.when(s == 3)
    def _():
        for m in range(MICRO):
            for c in range(C):
                ubuf[m, c, t] = seeds(m, c)

    @pl.when(s == 1)
    def _():
        for m in range(MICRO):
            for c in range(C):
                relay[m, c, t] = seeds(m, c)

    pl.semaphore_wait(barrier, (T - 1) + (C - 1) + T + middle + jnp.where(odd, 1, T))
    def spread_n():
        for m in range(MICRO):
            for c in range(C):
                spread(nbuf, m, c, s_n, r_n)

    def slices_over_dp():
        for m in range(MICRO):
            for k in range(1, C):
                j = dpeer(k)
                send(nstage.at[m, j], nslice.at[m, d, t], s_a.at[m], r_a.at[m], {"dp": j})

    def slices_over_tensor():
        for m in range(MICRO):
            wait_for(nslice.at[m, pl.ds(0, C - 1), 0], r_a.at[m])
            for q in range(1, C):
                owner = dpeer(q)
                for k in range(1, T):
                    send(nslice.at[m, owner, t], nslice.at[m, owner, t], s_x.at[m, 0], r_x.at[m, 0],
                         {"tensor": tpeer(k)})

    @pl.when(s == 3)
    def _():
        for c in range(C):
            spread(nbuf, 0, c, s_n, r_n)
        send_seeds(0)

    @pl.when(s == 1)
    def _():
        part = pl.ds(row, HALF)
        slices_over_dp()
        for m in range(MICRO):
            for c in range(C):
                spread_row(relay, m, c, s_l, r_l)
        for m in range(MICRO):
            for c in range(C):
                wait_for(relay.at[m, c, pl.ds(0, HALF - 1)], r_l.at[m, c])
                send(relay.at[m, c, part], ubuf.at[m, c, part], s_f.at[m, c], r_u.at[m, c],
                     {"section": cross, "tensor": facing})
        spread_n()
        slices_over_tensor()
        for m in range(MICRO):
            for c in range(C):
                wait_for(relay.at[m, c, pl.ds(0, HALF)], s_f.at[m, c])
        pl.semaphore_signal(go, inc=1, device_id={"section": mate}, device_id_type=MESH)

    @pl.when(s == 2)
    def _():
        for m in range(MICRO):
            for c in range(C):
                for k in range(T):
                    send(nstage.at[m, c], relay.at[m, c, t], s_l.at[m, c], r_l.at[m, c],
                         {"section": cross, "tensor": lax.rem(t + k, T)})

    @pl.when(s == 0)
    def _():
        slices_over_dp()
        for c in range(C):
            wait_for(relay.at[0, c], r_l.at[0, c])
        spread_n()
        slices_over_tensor()
        pl.semaphore_wait(go, 1)
        for m in range(MICRO):
            for c in range(C):
                if m > 0:
                    wait_for(relay.at[m, c], r_l.at[m, c])
                send(relay.at[m, c], nbuf.at[m, c], s_f.at[m, c], r_n.at[m, c],
                     {"section": cross, "tensor": facing})

    def down_load(c):
        slot = c % 2
        return pltpu.make_async_copy(wd_hbm.at[:, pl.ds(c * CH, CH)], wd.at[slot], s_d.at[slot])

    for c in range(C):
        down_load(c).wait()
        half = max(128, CH // 2)
        for n in range(CH // half):
            wdt[c * CH + n * half : c * CH + (n + 1) * half, :] = wd[c % 2, :, n * half : (n + 1) * half].T
        if c + 2 < C:
            down_load(c + 2).start()
    for load in loads:
        load.wait()

    def exchange_slices(buf, slices, which, m):
        for k in range(1, C):
            j = dpeer(k)
            send(buf.at[m, j], slices.at[m, d], s_x.at[m, which], r_x.at[m, which], {"dp": j})
        slices[m, d] = buf[m, d]

    def exchange_all(buf, which, m):
        for k in range(1, C):
            send(buf.at[m, d], buf.at[m, d], s_x.at[m, which], r_x.at[m, which], {"dp": dpeer(k)})

    def rows_of(buf, m, c):
        return buf[m, c].reshape(TOK, CH)

    def forward(m):
        total = jnp.zeros((TOK, 2 * F), F32)
        for c in range(C):
            @pl.when(s == 2)
            def _():
                wait_for(nbuf.at[m, c], r_n.at[m, c])

            @pl.when(s != 2)
            def _():
                wait_for(others(nbuf, m, c), r_n.at[m, c])
            if m == 0:
                @pl.when(s == 3)
                def _():
                    spread(nbuf, 1, c, s_n, r_n)
            total += dot(rows_of(nbuf, m, c), w2[c * CH : (c + 1) * CH, :], NN)
        pall[m, d] = total.astype(BF16)
        exchange_all(pall, 2, m)
        pre_up = total[:, F:]
        value, slope = gelu_parts(total[:, :F])
        act[m] = value
        ups[m] = pre_up * slope

        @pl.when(s >= 2)
        def _():
            exchange_slices(nbuf, nslice, 0, m)

        @pl.when(s < 2)
        def _():
            nslice[m, d] = nbuf[m, d]

    def expand(m):
        wait_for(pall.at[m, pl.ds(0, C - 1)], r_x.at[m, 2])
        wait_for(pall.at[m, pl.ds(0, C - 1)], s_x.at[m, 2])

        def one(j, carry):
            pre_gate = pall[m, j, :, :F].astype(F32)
            pre_up = pall[m, j, :, F:].astype(F32)
            value, slope = gelu_parts(pre_gate)
            hall[m, j] = (value * pre_up).astype(BF16)
            pall[m, j, :, :F] = (pre_up * slope).astype(BF16)
            pall[m, j, :, F:] = value.astype(BF16)
            return carry

        lax.fori_loop(0, C, one, 0)

    def expand_grads(m):
        def one(j, carry):
            upstream = hgrad[m, j]
            gall[m, j, :, :F] = upstream * pall[m, j, :, :F]
            gall[m, j, :, F:] = upstream * pall[m, j, :, F:]
            return carry

        lax.fori_loop(0, C, one, 0)

    def products(m):
        grad_hidden = jnp.zeros((TOK, F), F32)
        for c in range(C):
            @pl.when(odd)
            def _():
                wait_for(others(ubuf, m, c), r_u.at[m, c])

            @pl.when(jnp.logical_not(odd))
            def _():
                wait_for(ubuf.at[m, c], r_u.at[m, c])
            if m == 0:
                @pl.when(s == 3)
                def _():
                    spread_row(ubuf, 1, c, s_u, r_u)
            grad_hidden += dot(rows_of(ubuf, m, c), wdt[c * CH : (c + 1) * CH, :], NN)
        exchange_slices(ubuf, uslice, 1, m)
        hgrad[m, d] = grad_hidden.astype(BF16)
        exchange_all(hgrad, 3, m)
        both = jnp.concatenate(
            [(grad_hidden * ups[m]).astype(BF16), (grad_hidden * act[m]).astype(BF16)], axis=1
        )
        for c in range(C):
            term = dot(both, w2[c * CH : (c + 1) * CH, :], NT).astype(BF16)
            pbuf[m, c] = term.reshape(T, R, CH)
            rbuf[m, c, t] = pbuf[m, c, t]
            for k in range(1, T):
                j = tpeer(k)
                send(pbuf.at[m, c, j], rbuf.at[m, c, t], s_p.at[m, c], r_p.at[m, c], {"tensor": j})
    def finish(m):
        inv = inv_buf[m, :, 0:1]
        mean = jnp.zeros((R, 1), F32)
        sums = []
        for c in range(C):
            cols = slice(c * CH, (c + 1) * CH)
            wait_for(others(rbuf, m, c), r_p.at[m, c])
            grad_normed = jnp.zeros((R, CH), F32)
            for j in range(T):
                grad_normed += rbuf[m, c, j].astype(F32)
            part = x_ref[m, :, cols].astype(F32)
            scaled = grad_normed * gain_ref[:, cols]
            mean += jnp.sum(scaled * part, axis=-1, keepdims=True)
            gain_part = jnp.sum(grad_normed * part * inv, axis=0, keepdims=True)
            if m == 0:
                gsum[:, cols] = gain_part
            else:
                gsum[:, cols] += gain_part
            sums.append(scaled)
        factor = inv * inv * inv * (mean * (1.0 / D))
        for c in range(C):
            cols = slice(c * CH, (c + 1) * CH)
            part = x_ref[m, :, cols].astype(F32)
            result = ubuf[m, c, t].astype(F32) + inv * sums[c] - part * factor
            rows = result.astype(BF16)
            obuf[m, c] = rows
            orow_ref[m, :, cols] = rows

            @pl.when(odd)
            def _():
                for k in range(T):
                    send(obuf.at[m, c], ubuf.at[m, c, t], s_o.at[m, c], r_u.at[m, c],
                         {"section": s - 1, "tensor": lax.rem(t + k, T)})

            @pl.when(s == 2)
            def _():
                send(obuf.at[m, c], ubuf.at[m, c, t], s_o.at[m, c], r_hop.at[m, c], {"section": s - 1})

    forward(0)
    pl.when(s < 2)(lambda: forward(1))

    @pl.when(s == 1)
    def _():
        for m in range(MICRO):
            for c in range(C):
                wait_for(ubuf.at[m, c, t], r_hop.at[m, c])
                spread(ubuf, m, c, s_u, r_u)

    @pl.when(s == 0)
    def _():
        for m in range(MICRO):
            expand(m)

    products(0)
    pl.when(s >= 2)(lambda: forward(1))
    products(1)

    finish(0)

    count = C * TOK
    step = min(256, CH)

    def slices_arrived(m):
        @pl.when(s >= 2)
        def _():
            wait_for(nslice.at[m, pl.ds(0, C - 1)], r_x.at[m, 0])

        @pl.when(s < 2)
        def _():
            wait_for(nslice.at[m, pl.ds(0, C - 1), pl.ds(0, T - 1)], r_x.at[m, 0])

        wait_for(uslice.at[m, pl.ds(0, C - 1)], r_x.at[m, 1])

    def grads_arrived(m):
        wait_for(hgrad.at[m, pl.ds(0, C - 1)], r_x.at[m, 3])
        expand_grads(m)

    def term_down(m, cols):
        return dot(hall[m].reshape(count, F), uslice[m, :, :, :, cols].reshape(count, step), TN)

    def first_terms():
        slices_arrived(0)
        for n in range(CH // step):
            cols = slice(n * step, (n + 1) * step)
            accd[:, cols] = term_down(0, cols)
        grads_arrived(0)
        for n in range(CH // step):
            part = slice(n * step, (n + 1) * step)
            accg[part, :] = gate_up_term(nslice, gall, 0, part)

    pl.when(s == 0)(first_terms)
    finish(1)

    gten[t] = gsum[...]
    for k in range(1, T):
        send(gsum, gten.at[t], s_gain.at[0], r_gain.at[0], {"tensor": tpeer(k)})

    @pl.when(s > 0)
    def _():
        for m in range(MICRO):
            expand(m)

    pl.when(s > 0)(first_terms)
    slices_arrived(1)
    for n in range(CH // step):
        cols = slice(n * step, (n + 1) * step)
        od_ref[:, cols] = (accd[:, cols] + term_down(1, cols)).astype(BF16)

    wait_for(gten.at[pl.ds(0, T - 1)], r_gain.at[0])
    gain_total = gten[0]
    for j in range(1, T):
        gain_total += gten[j]
    gdp_in[...] = gain_total
    gdp[d] = gain_total
    for k in range(1, C):
        send(gdp_in, gdp.at[d], s_gain.at[1], r_gain.at[1], {"dp": dpeer(k)})

    grads_arrived(1)

    wait_for(gdp.at[pl.ds(0, C - 1)], r_gain.at[1])
    gain_total = gdp[0]
    for j in range(1, C):
        gain_total += gdp[j]
    ogain_ref[...] = gain_total

    for m in range(MICRO):
        for c in range(C):
            wait_for(others(pbuf, m, c), s_p.at[m, c])

            @pl.when(odd)
            def _():
                wait_for(ubuf.at[m, c], s_o.at[m, c])

            @pl.when(s == 0)
            def _():
                wait_for(relay.at[m, c], s_f.at[m, c])

            @pl.when(s == 1)
            def _():
                wait_for(relay.at[m, c, pl.ds(0, HALF - 1)], s_l.at[m, c])
                wait_for(others(ubuf, m, c), s_u.at[m, c])

            @pl.when(s == 3)
            def _():
                wait_for(ubuf.at[m, c, pl.ds(0, HALF - 1)], s_u.at[m, c])

            @pl.when(s != 2)
            def _():
                wait_for(others(nbuf, m, c), s_n.at[m, c])

            @pl.when(s == 2)
            def _():
                wait_for(relay.at[m, c], s_l.at[m, c])
                wait_for(obuf.at[m, c], s_o.at[m, c])
        @pl.when(s >= 2)
        def _():
            wait_for(nslice.at[m, pl.ds(0, C - 1)], s_x.at[m, 0])

        @pl.when(s < 2)
        def _():
            wait_for(nslice.at[m, pl.ds(0, C - 1), 0], s_a.at[m])
            wait_for(nslice.at[m, pl.ds(0, C - 1), pl.ds(0, T - 1)], s_x.at[m, 0])

        wait_for(uslice.at[m, pl.ds(0, C - 1)], s_x.at[m, 1])
        wait_for(hgrad.at[m, pl.ds(0, C - 1)], s_x.at[m, 3])
    wait_for(gten.at[pl.ds(0, T - 1)], s_gain.at[0])
    wait_for(gdp.at[pl.ds(0, C - 1)], s_gain.at[1])


def gate_up_term(nslice, gall, m, rows):
    C, T, R, _ = nslice.shape[1:]
    step = rows.stop - rows.start
    left = nslice[m, :, :, :, rows].reshape(C * T * R, step)
    return dot(left, gall[m].reshape(C * T * R, gall.shape[-1]), TN)


def writer(down, gain, rows, accg, nslice, gall, og, ou, od, ogain, orow, vg, vu, sems, tile_sems):
    copies = [
        pltpu.make_async_copy(down, od, sems.at[0]),
        pltpu.make_async_copy(gain, ogain, sems.at[1]),
        pltpu.make_async_copy(rows, orow, sems.at[2]),
    ]
    for copy in copies:
        copy.start()
    CH, F = vg.shape
    step = min(256, CH)
    for n in range(CH // step):
        part = slice(n * step, (n + 1) * step)
        total = accg[part, :] + gate_up_term(nslice, gall, MICRO - 1, part)
        vg[part, :] = total[:, :F].astype(BF16)
        vu[part, :] = total[:, F:].astype(BF16)
        for which, (src, dst) in enumerate(((vg, og), (vu, ou))):
            block = pl.ds(n * step, step)
            copy = pltpu.make_async_copy(src.at[block], dst.at[block], tile_sems.at[which, n])
            copy.start()
            copies.append(copy)
    for copy in copies:
        copy.wait()


def body(T, C, section_inputs, gain, w_gate, w_up, w_down, cotangent, lengths):
    _, micro, R, D = section_inputs.shape
    F = w_gate.shape[2]
    CH = D // C
    TOK = T * R
    dims = (T, C, R, F, CH)
    vmem = pl.BlockSpec(memory_space=pltpu.VMEM)
    smem = pl.BlockSpec(memory_space=pltpu.SMEM)
    hbm = pl.BlockSpec(memory_space=pl.ANY)
    dma = pltpu.SemaphoreType.DMA
    flops = 2 * micro * 8 * TOK * D * F
    outs = pl.pallas_call(
        functools.partial(kernel, dims),
        out_shape=(
            pltpu.VMEM((F, CH), BF16),
            pltpu.VMEM((1, D), F32),
            pltpu.VMEM((micro, R, D), BF16),
            pltpu.VMEM((CH, 2 * F), F32),
            pltpu.VMEM((micro, C, T, R, CH), BF16),
            pltpu.VMEM((micro, C, TOK, 2 * F), BF16),
        ),
        in_specs=[smem] + [hbm] * 6,
        out_specs=(vmem,) * 6,
        scratch_shapes=[
            pltpu.VMEM((micro, R, D), BF16),
            pltpu.VMEM((1, D), F32),
            pltpu.VMEM((micro, R, D), BF16),
            pltpu.VMEM((D, 2 * F), BF16),
            pltpu.VMEM((2, F, CH), BF16),
            pltpu.VMEM((D, F), BF16),
            pltpu.VMEM((micro, C, T, R, CH), BF16),
            pltpu.VMEM((micro, C, T, R, CH), BF16),
            pltpu.VMEM((micro, C, T, R, CH), BF16),
            pltpu.VMEM((micro, C, T, R, CH), BF16),
            pltpu.VMEM((micro, C, R, CH), BF16),
            pltpu.VMEM((micro, C, R, CH), BF16),
            pltpu.VMEM((micro, C, T, R, CH), BF16),
            pltpu.VMEM((micro, C, T, R, CH), BF16),
            pltpu.VMEM((micro, C, TOK, 2 * F), BF16),
            pltpu.VMEM((micro, C, TOK, F), BF16),
            pltpu.VMEM((micro, C, TOK, F), BF16),
            pltpu.VMEM((micro, TOK, F), F32),
            pltpu.VMEM((micro, TOK, F), F32),
            pltpu.VMEM((micro, R, 128), F32),
            pltpu.VMEM((F, CH), F32),
            pltpu.VMEM((1, D), F32),
            pltpu.VMEM((T, 1, D), F32),
            pltpu.VMEM((1, D), F32),
            pltpu.VMEM((C, 1, D), F32),
            dma((6,)),
            dma((2,)),
            dma((micro, C)),
            dma((micro, C)),
            dma((micro, C)),
            dma((micro, C)),
            dma((micro, C)),
            dma((micro, C)),
            dma((micro, C)),
            dma((micro, C)),
            dma((micro, C)),
            dma((micro, C)),
            dma((micro, C)),
            dma((micro,)),
            dma((micro,)),
            dma((micro, 4)),
            dma((micro, 4)),
            dma((2,)),
            dma((2,)),
            pltpu.SemaphoreType.REGULAR,
        ],
        cost_estimate=pl.CostEstimate(
            flops=flops, bytes_accessed=24 * D * F // 2, transcendentals=micro * TOK * F
        ),
        compiler_params=pltpu.CompilerParams(
            collective_id=0, has_side_effects=True, vmem_limit_bytes=46 * 1024 * 1024
        ),
    )(lengths, section_inputs[0], gain, cotangent, w_gate[0], w_up[0], w_down[0])
    gate, up, down, gain_out, rows = pl.pallas_call(
        writer,
        out_shape=(
            jax.ShapeDtypeStruct((CH, F), BF16),
            jax.ShapeDtypeStruct((CH, F), BF16),
            jax.ShapeDtypeStruct((F, CH), BF16),
            jax.ShapeDtypeStruct((1, D), F32),
            jax.ShapeDtypeStruct((micro, R, D), BF16),
        ),
        in_specs=[vmem] * len(outs),
        out_specs=(hbm,) * 5,
        scratch_shapes=[
            pltpu.VMEM((CH, F), BF16),
            pltpu.VMEM((CH, F), BF16),
            dma((3,)),
            dma((2, max(1, CH // 256))),
        ],
        compiler_params=pltpu.CompilerParams(vmem_limit_bytes=14 * 1024 * 1024),
    )(*outs)
    return (gate[None], up[None], down[None], gain_out, rows[None])


def solution(mesh):
    T, C = mesh.shape["tensor"], mesh.shape["dp"]
    in_specs = (
        P("section", None, ("dp", "tensor"), None),
        P("section", None),
        P("section", None, "tensor"),
        P("section", None, "tensor"),
        P("section", "tensor", None),
        P(None, ("dp", "tensor"), None),
        P(None, "dp"),
    )
    out_specs = (
        P("section", "dp", "tensor"),
        P("section", "dp", "tensor"),
        P("section", "tensor", "dp"),
        P("section", None),
        P("section", None, ("dp", "tensor"), None),
    )
    return jax.shard_map(
        functools.partial(body, T, C), mesh=mesh, in_specs=in_specs, out_specs=out_specs, check_vma=False
    )
```

```python
import functools
import math

import jax
import jax.numpy as jnp
from jax import lax
from jax.experimental import pallas as pl
from jax.experimental.pallas import tpu as pltpu
from jax.sharding import PartitionSpec as P

EPSILON = 1e-06
GELU_SCALE = math.sqrt(2.0 / math.pi)
GELU_CUBIC = 0.044715
MESH = pl.DeviceIdType.MESH
F32 = jnp.float32
BF16 = jnp.bfloat16
MICRO = 2
NN = (((1,), (0,)), ((), ()))
NT = (((1,), (1,)), ((), ()))
TN = (((0,), (0,)), ((), ()))


def dot(a, b, dims):
    return lax.dot_general(a, b, dims, preferred_element_type=F32)


def gelu_parts(pre_gate):
    tanh_arg = GELU_SCALE * (pre_gate + GELU_CUBIC * pre_gate * pre_gate * pre_gate)
    tanh_part = jnp.tanh(tanh_arg)
    gelu_value = 0.5 * pre_gate * (1.0 + tanh_part)
    gelu_slope = 0.5 * (1.0 + tanh_part) + 0.5 * pre_gate * (
        1.0 - tanh_part * tanh_part
    ) * GELU_SCALE * (1.0 + 3.0 * GELU_CUBIC * pre_gate * pre_gate)
    return (gelu_value, gelu_slope)


def kernel(
    dims,
    len_ref, x_hbm, gain_hbm, cot_hbm, wg_hbm, wu_hbm, wd_hbm,
    od_ref, ogain_ref, orow_ref, accg, nslice, pall,
    x_ref, gain_ref, cot_ref, w2, w2t, wd, wdt, nbuf, ubuf, pbuf, rbuf, obuf, nstage, relay, uslice, hgrad, hall, act, ups, inv_buf,
    accd, gsum, gten, gdp_in, gdp,
    s_w, s_d, s_n, r_n, s_u, r_u, s_p, r_p, s_o, r_hop, s_l, r_l, s_f, s_a, r_a, s_x, r_x, s_gain, r_gain, go,
):
    T, C, R, F, CH = dims
    D = C * CH
    TOK = T * R
    HALF = T // 2
    s = lax.axis_index("section")
    t = lax.axis_index("tensor")
    d = lax.axis_index("dp")

    rings = sorted(range(HALF), key=lambda q: -min(q, HALF - q))
    offsets = [(dy, dz) for dz in rings for dy in (1, 0)]
    line = t // HALF
    place = lax.rem(t, HALF)

    def tpeer(k):
        dy, dz = offsets[k - 1]
        return (1 - line if dy else line) * HALF + lax.rem(place + dz, HALF)

    def dpeer(k):
        return lax.rem(d + k, C)

    barrier = pltpu.get_barrier_semaphore()

    def greet(where):
        pl.semaphore_signal(barrier, inc=1, device_id=where, device_id_type=MESH)

    for k in range(1, T):
        greet({"tensor": tpeer(k)})
    for k in range(1, C):
        greet({"dp": dpeer(k)})
    mate = s + 1 - 2 * lax.rem(s, 2)
    for k in range(T):
        greet({"section": mate, "tensor": lax.rem(t + k, T)})

    @pl.when(s == 1)
    def _():
        greet({"section": 2})

    @pl.when(s == 2)
    def _():
        greet({"section": 1})

    cross = lax.rem(s + 2, 4)
    facing = lax.rem(t + HALF, T)
    odd = lax.rem(s, 2) == 1

    @pl.when(odd)
    def _():
        greet({"section": cross, "tensor": facing})

    @pl.when(jnp.logical_not(odd))
    def _():
        for k in range(T):
            greet({"section": cross, "tensor": lax.rem(t + k, T)})

    middle = jnp.where((s == 1) | (s == 2), 1, 0)

    def send(src, dst, ssem, rsem, where):
        pltpu.make_async_remote_copy(
            src_ref=src, dst_ref=dst, send_sem=ssem, recv_sem=rsem,
            device_id=where, device_id_type=MESH,
        ).start()

    def wait_for(ref, sem):
        pltpu.make_async_copy(ref, ref, sem).wait()

    def spread(buf, m, c, ssem, rsem):
        for k in range(1, T):
            send(buf.at[m, c, t], buf.at[m, c, t], ssem.at[m, c], rsem.at[m, c], {"tensor": tpeer(k)})

    def others(buf, m, c):
        return buf.at[m, c, pl.ds(0, T - 1)]

    inputs = [
        pltpu.make_async_copy(x_hbm, x_ref, s_w.at[3]),
        pltpu.make_async_copy(gain_hbm, gain_ref, s_w.at[4]),
        pltpu.make_async_copy(cot_hbm, cot_ref, s_w.at[5]),
    ]
    for load in inputs:
        load.start()
    loads = [
        pltpu.make_async_copy(wg_hbm, w2.at[:, pl.ds(0, F)], s_w.at[0]),
        pltpu.make_async_copy(wu_hbm, w2.at[:, pl.ds(F, F)], s_w.at[1]),
    ]
    for load in loads:
        load.start()
    lead = max(128, CH // 4)
    for n in range(2):
        pltpu.make_async_copy(wd_hbm.at[:, pl.ds(n * lead, lead)], wd.at[n], s_d.at[n]).start()

    for load in inputs:
        load.wait()

    keep_pos = lax.broadcasted_iota(jnp.int32, (R, 1), 0)
    for m in range(MICRO):
        square = jnp.zeros((R, 1), F32)
        for c in range(C):
            part = x_ref[m, :, c * CH : (c + 1) * CH].astype(F32)
            square += jnp.sum(part * part, axis=-1, keepdims=True)
        inv = lax.rsqrt(square * (1.0 / D) + EPSILON)
        inv_buf[m] = jnp.broadcast_to(inv, (R, 128))
        for c in range(C):
            cols = slice(c * CH, (c + 1) * CH)
            rows = (x_ref[m, :, cols].astype(F32) * inv * gain_ref[:, cols]).astype(BF16)
            nstage[m, c] = rows

            @pl.when(s != 2)
            def _():
                nbuf[m, c, t] = rows

    def seeds(m, c):
        keep = (keep_pos < len_ref[m, t]).astype(F32)
        return (cot_ref[m, :, c * CH : (c + 1) * CH].astype(F32) * keep).astype(BF16)

    row = (t // HALF) * HALF

    def rowpeer(k):
        return row + lax.rem(t - row + k, HALF)

    def spread_row(buf, m, c, ssem, rsem):
        for k in range(1, HALF):
            send(buf.at[m, c, t], buf.at[m, c, t], ssem.at[m, c], rsem.at[m, c], {"tensor": rowpeer(k)})

    def send_seeds(m):
        for c in range(C):
            spread_row(ubuf, m, c, s_u, r_u)

    @pl.when(s == 3)
    def _():
        for m in range(MICRO):
            for c in range(C):
                ubuf[m, c, t] = seeds(m, c)

    @pl.when(s == 1)
    def _():
        for m in range(MICRO):
            for c in range(C):
                relay[m, c, t] = seeds(m, c)

    pl.semaphore_wait(barrier, (T - 1) + (C - 1) + T + middle + jnp.where(odd, 1, T))
    def spread_n():
        for m in range(MICRO):
            for c in range(C):
                spread(nbuf, m, c, s_n, r_n)

    def slices_over_dp():
        for m in range(MICRO):
            for k in range(1, C):
                j = dpeer(k)
                send(nstage.at[m, j], nslice.at[m, d, t], s_a.at[m], r_a.at[m], {"dp": j})

    def slices_over_tensor():
        for m in range(MICRO):
            wait_for(nslice.at[m, pl.ds(0, C - 1), 0], r_a.at[m])
            for q in range(1, C):
                owner = dpeer(q)
                for k in range(1, T):
                    send(nslice.at[m, owner, t], nslice.at[m, owner, t], s_x.at[m, 0], r_x.at[m, 0],
                         {"tensor": tpeer(k)})

    @pl.when(s == 3)
    def _():
        for c in range(C):
            spread(nbuf, 0, c, s_n, r_n)
        send_seeds(0)

    @pl.when(s == 1)
    def _():
        part = pl.ds(row, HALF)
        slices_over_dp()
        for m in range(MICRO):
            for c in range(C):
                spread_row(relay, m, c, s_l, r_l)
        for m in range(MICRO):
            for c in range(C):
                wait_for(relay.at[m, c, pl.ds(0, HALF - 1)], r_l.at[m, c])
                send(relay.at[m, c, part], ubuf.at[m, c, part], s_f.at[m, c], r_u.at[m, c],
                     {"section": cross, "tensor": facing})
        spread_n()
        slices_over_tensor()
        for m in range(MICRO):
            for c in range(C):
                wait_for(relay.at[m, c, pl.ds(0, HALF)], s_f.at[m, c])
        pl.semaphore_signal(go, inc=1, device_id={"section": mate}, device_id_type=MESH)

    @pl.when(s == 2)
    def _():
        for m in range(MICRO):
            for c in range(C):
                for k in range(T):
                    send(nstage.at[m, c], relay.at[m, c, t], s_l.at[m, c], r_l.at[m, c],
                         {"section": cross, "tensor": lax.rem(t + k, T)})

    @pl.when(s == 0)
    def _():
        slices_over_dp()
        for c in range(C):
            wait_for(relay.at[0, c], r_l.at[0, c])
        spread_n()
        slices_over_tensor()
        pl.semaphore_wait(go, 1)
        for m in range(MICRO):
            for c in range(C):
                if m > 0:
                    wait_for(relay.at[m, c], r_l.at[m, c])
                send(relay.at[m, c], nbuf.at[m, c], s_f.at[m, c], r_n.at[m, c],
                     {"section": cross, "tensor": facing})

    half = max(128, CH // 4)
    pieces = D // half

    def down_load(n):
        return pltpu.make_async_copy(wd_hbm.at[:, pl.ds(n * half, half)], wd.at[n % 2], s_d.at[n % 2])

    for n in range(pieces):
        down_load(n).wait()
        wdt[n * half : (n + 1) * half, :] = wd[n % 2].T
        if n + 2 < pieces:
            down_load(n + 2).start()
    for load in loads:
        load.wait()

    def exchange_slices(buf, slices, which, m):
        for k in range(1, C):
            j = dpeer(k)
            send(buf.at[m, j], slices.at[m, d], s_x.at[m, which], r_x.at[m, which], {"dp": j})
        slices[m, d] = buf[m, d]

    def exchange_all(buf, which, m):
        for k in range(1, C):
            send(buf.at[m, d], buf.at[m, d], s_x.at[m, which], r_x.at[m, which], {"dp": dpeer(k)})

    def rows_of(buf, m, c):
        return buf[m, c].reshape(TOK, CH)

    def forward(m):
        total = jnp.zeros((TOK, 2 * F), F32)
        for c in range(C):
            @pl.when(s == 2)
            def _():
                wait_for(nbuf.at[m, c], r_n.at[m, c])

            @pl.when(s != 2)
            def _():
                wait_for(others(nbuf, m, c), r_n.at[m, c])
            if m == 0:
                @pl.when(s == 3)
                def _():
                    spread(nbuf, 1, c, s_n, r_n)
            total += dot(rows_of(nbuf, m, c), w2[c * CH : (c + 1) * CH, :], NN)
            if m == 0:
                for n in range(CH // half):
                    part = slice(c * CH + n * half, c * CH + (n + 1) * half)
                    w2t[:, part] = w2[part, :].T
        pall[m, d] = total.astype(BF16)
        exchange_all(pall, 2, m)
        pre_up = total[:, F:]
        value, slope = gelu_parts(total[:, :F])
        act[m] = value
        ups[m] = pre_up * slope

        @pl.when(s >= 2)
        def _():
            exchange_slices(nbuf, nslice, 0, m)

        @pl.when(s < 2)
        def _():
            nslice[m, d] = nbuf[m, d]

    def expand(m):
        wait_for(pall.at[m, pl.ds(0, C - 1)], r_x.at[m, 2])
        wait_for(pall.at[m, pl.ds(0, C - 1)], s_x.at[m, 2])

        def one(j, carry):
            pre_gate = pall[m, j, :, :F].astype(F32)
            pre_up = pall[m, j, :, F:].astype(F32)
            value, slope = gelu_parts(pre_gate)
            hall[m, j] = (value * pre_up).astype(BF16)
            pall[m, j, :, :F] = (pre_up * slope).astype(BF16)
            pall[m, j, :, F:] = value.astype(BF16)
            return carry

        lax.fori_loop(0, C, one, 0)

    def expand_grads(m):
        def one(j, carry):
            upstream = hgrad[m, j]
            pall[m, j, :, :F] = upstream * pall[m, j, :, :F]
            pall[m, j, :, F:] = upstream * pall[m, j, :, F:]
            return carry

        lax.fori_loop(0, C, one, 0)

    def products(m):
        grad_hidden = jnp.zeros((TOK, F), F32)
        for c in range(C):
            @pl.when(odd)
            def _():
                wait_for(others(ubuf, m, c), r_u.at[m, c])

            @pl.when(jnp.logical_not(odd))
            def _():
                wait_for(ubuf.at[m, c], r_u.at[m, c])
            if m == 0:
                @pl.when(s == 3)
                def _():
                    spread_row(ubuf, 1, c, s_u, r_u)
            grad_hidden += dot(rows_of(ubuf, m, c), wdt[c * CH : (c + 1) * CH, :], NN)
        exchange_slices(ubuf, uslice, 1, m)
        hgrad[m, d] = grad_hidden.astype(BF16)
        exchange_all(hgrad, 3, m)
        both = jnp.concatenate(
            [(grad_hidden * ups[m]).astype(BF16), (grad_hidden * act[m]).astype(BF16)], axis=1
        )
        for c in range(C):
            term = dot(both, w2t[:, c * CH : (c + 1) * CH], NN).astype(BF16)
            pbuf[m, c] = term.reshape(T, R, CH)
            rbuf[m, c, t] = pbuf[m, c, t]
            for k in range(1, T):
                j = tpeer(k)
                send(pbuf.at[m, c, j], rbuf.at[m, c, t], s_p.at[m, c], r_p.at[m, c], {"tensor": j})
    def send_gain():
        for k in range(1, T):
            send(gsum, gten.at[t], s_gain.at[0], r_gain.at[0], {"tensor": tpeer(k)})

    def finish(m):
        inv = inv_buf[m, :, 0:1]
        mean = jnp.zeros((R, 1), F32)
        sums = []
        for c in range(C):
            cols = slice(c * CH, (c + 1) * CH)
            wait_for(others(rbuf, m, c), r_p.at[m, c])
            grad_normed = jnp.zeros((R, CH), F32)
            for j in range(T):
                grad_normed += rbuf[m, c, j].astype(F32)
            part = x_ref[m, :, cols].astype(F32)
            scaled = grad_normed * gain_ref[:, cols]
            mean += jnp.sum(scaled * part, axis=-1, keepdims=True)
            gain_part = jnp.sum(grad_normed * part * inv, axis=0, keepdims=True)
            if m == 0:
                gsum[:, cols] = gain_part
            else:
                gsum[:, cols] += gain_part
            sums.append(scaled)
        if m == MICRO - 1:
            pl.when(s == 0)(send_gain)
        factor = inv * inv * inv * (mean * (1.0 / D))
        for c in range(C):
            cols = slice(c * CH, (c + 1) * CH)
            part = x_ref[m, :, cols].astype(F32)
            result = ubuf[m, c, t].astype(F32) + inv * sums[c] - part * factor
            rows = result.astype(BF16)
            obuf[m, c] = rows
            orow_ref[m, :, cols] = rows

            @pl.when(odd)
            def _():
                for k in range(1, T + 1):
                    send(obuf.at[m, c], ubuf.at[m, c, t], s_o.at[m, c], r_u.at[m, c],
                         {"section": s - 1, "tensor": tpeer(k)})

            @pl.when(s == 2)
            def _():
                send(obuf.at[m, c], ubuf.at[m, c, t], s_o.at[m, c], r_hop.at[m, c], {"section": s - 1})

    forward(0)
    pl.when(s < 2)(lambda: forward(1))

    @pl.when(s == 1)
    def _():
        for m in range(MICRO):
            for c in range(C):
                wait_for(ubuf.at[m, c, t], r_hop.at[m, c])
                spread(ubuf, m, c, s_u, r_u)

    @pl.when(s == 0)
    def _():
        for m in range(MICRO):
            expand(m)

    products(0)
    pl.when(s >= 2)(lambda: forward(1))
    products(1)

    finish(0)

    count = C * TOK
    step = min(256, CH)

    def slices_arrived(m):
        @pl.when(s >= 2)
        def _():
            wait_for(nslice.at[m, pl.ds(0, C - 1)], r_x.at[m, 0])

        @pl.when(s < 2)
        def _():
            wait_for(nslice.at[m, pl.ds(0, C - 1), pl.ds(0, T - 1)], r_x.at[m, 0])

        wait_for(uslice.at[m, pl.ds(0, C - 1)], r_x.at[m, 1])

    def grads_arrived(m):
        wait_for(hgrad.at[m, pl.ds(0, C - 1)], r_x.at[m, 3])
        expand_grads(m)

    def term_down(m, cols):
        return dot(hall[m].reshape(count, F), uslice[m, :, :, :, cols].reshape(count, step), TN)

    def first_terms():
        slices_arrived(0)
        for n in range(CH // step):
            cols = slice(n * step, (n + 1) * step)
            accd[:, cols] = term_down(0, cols)
        grads_arrived(0)
        for n in range(CH // step):
            part = slice(n * step, (n + 1) * step)
            accg[part, :] = gate_up_term(nslice, pall, 0, part)

    pl.when(s == 0)(first_terms)
    finish(1)

    gten[t] = gsum[...]
    pl.when(s > 0)(send_gain)

    @pl.when(s > 0)
    def _():
        for m in range(MICRO):
            expand(m)

    pl.when(s > 0)(first_terms)
    slices_arrived(1)
    for n in range(CH // step):
        cols = slice(n * step, (n + 1) * step)
        od_ref[:, cols] = (accd[:, cols] + term_down(1, cols)).astype(BF16)

    wait_for(gten.at[pl.ds(0, T - 1)], r_gain.at[0])
    gain_total = gten[0]
    for j in range(1, T):
        gain_total += gten[j]
    gdp_in[...] = gain_total
    gdp[d] = gain_total
    for k in range(1, C):
        send(gdp_in, gdp.at[d], s_gain.at[1], r_gain.at[1], {"dp": dpeer(k)})

    grads_arrived(1)

    for m in range(MICRO):
        for c in range(C):
            wait_for(others(pbuf, m, c), s_p.at[m, c])

            @pl.when(odd)
            def _():
                wait_for(ubuf.at[m, c], s_o.at[m, c])

            @pl.when(s == 0)
            def _():
                wait_for(relay.at[m, c], s_f.at[m, c])

            @pl.when(s == 1)
            def _():
                wait_for(relay.at[m, c, pl.ds(0, HALF - 1)], s_l.at[m, c])
                wait_for(others(ubuf, m, c), s_u.at[m, c])

            @pl.when(s == 3)
            def _():
                wait_for(ubuf.at[m, c, pl.ds(0, HALF - 1)], s_u.at[m, c])

            @pl.when(s != 2)
            def _():
                wait_for(others(nbuf, m, c), s_n.at[m, c])

            @pl.when(s == 2)
            def _():
                wait_for(relay.at[m, c], s_l.at[m, c])
                wait_for(obuf.at[m, c], s_o.at[m, c])
        @pl.when(s >= 2)
        def _():
            wait_for(nslice.at[m, pl.ds(0, C - 1)], s_x.at[m, 0])

        @pl.when(s < 2)
        def _():
            wait_for(nslice.at[m, pl.ds(0, C - 1), 0], s_a.at[m])
            wait_for(nslice.at[m, pl.ds(0, C - 1), pl.ds(0, T - 1)], s_x.at[m, 0])

        wait_for(uslice.at[m, pl.ds(0, C - 1)], s_x.at[m, 1])
        wait_for(hgrad.at[m, pl.ds(0, C - 1)], s_x.at[m, 3])
    wait_for(gdp.at[pl.ds(0, C - 1)], r_gain.at[1])
    gain_total = gdp[0]
    for j in range(1, C):
        gain_total += gdp[j]
    ogain_ref[...] = gain_total
    wait_for(gten.at[pl.ds(0, T - 1)], s_gain.at[0])
    wait_for(gdp.at[pl.ds(0, C - 1)], s_gain.at[1])


def gate_up_term(nslice, gall, m, rows):
    C, T, R, _ = nslice.shape[1:]
    step = rows.stop - rows.start
    left = nslice[m, :, :, :, rows].reshape(C * T * R, step)
    return dot(left, gall[m].reshape(C * T * R, gall.shape[-1]), TN)


def writer(down, gain, rows, accg, nslice, gall, og, ou, od, ogain, orow, vg, vu, sems, tile_sems):
    copies = [
        pltpu.make_async_copy(down, od, sems.at[0]),
        pltpu.make_async_copy(gain, ogain, sems.at[1]),
        pltpu.make_async_copy(rows, orow, sems.at[2]),
    ]
    for copy in copies:
        copy.start()
    CH, F = vg.shape
    step = min(256, CH)
    for n in range(CH // step):
        part = slice(n * step, (n + 1) * step)
        total = accg[part, :] + gate_up_term(nslice, gall, MICRO - 1, part)
        vg[part, :] = total[:, :F].astype(BF16)
        vu[part, :] = total[:, F:].astype(BF16)
        for which, (src, dst) in enumerate(((vg, og), (vu, ou))):
            block = pl.ds(n * step, step)
            copy = pltpu.make_async_copy(src.at[block], dst.at[block], tile_sems.at[which, n])
            copy.start()
            copies.append(copy)
    for copy in copies:
        copy.wait()


def body(T, C, section_inputs, gain, w_gate, w_up, w_down, cotangent, lengths):
    _, micro, R, D = section_inputs.shape
    F = w_gate.shape[2]
    CH = D // C
    TOK = T * R
    dims = (T, C, R, F, CH)
    vmem = pl.BlockSpec(memory_space=pltpu.VMEM)
    smem = pl.BlockSpec(memory_space=pltpu.SMEM)
    hbm = pl.BlockSpec(memory_space=pl.ANY)
    dma = pltpu.SemaphoreType.DMA
    flops = 2 * micro * 8 * TOK * D * F
    outs = pl.pallas_call(
        functools.partial(kernel, dims),
        out_shape=(
            pltpu.VMEM((F, CH), BF16),
            pltpu.VMEM((1, D), F32),
            pltpu.VMEM((micro, R, D), BF16),
            pltpu.VMEM((CH, 2 * F), F32),
            pltpu.VMEM((micro, C, T, R, CH), BF16),
            pltpu.VMEM((micro, C, TOK, 2 * F), BF16),
        ),
        in_specs=[smem] + [hbm] * 6,
        out_specs=(vmem,) * 6,
        scratch_shapes=[
            pltpu.VMEM((micro, R, D), BF16),
            pltpu.VMEM((1, D), F32),
            pltpu.VMEM((micro, R, D), BF16),
            pltpu.VMEM((D, 2 * F), BF16),
            pltpu.VMEM((2 * F, D), BF16),
            pltpu.VMEM((2, F, max(128, CH // 4)), BF16),
            pltpu.VMEM((D, F), BF16),
            pltpu.VMEM((micro, C, T, R, CH), BF16),
            pltpu.VMEM((micro, C, T, R, CH), BF16),
            pltpu.VMEM((micro, C, T, R, CH), BF16),
            pltpu.VMEM((micro, C, T, R, CH), BF16),
            pltpu.VMEM((micro, C, R, CH), BF16),
            pltpu.VMEM((micro, C, R, CH), BF16),
            pltpu.VMEM((micro, C, T, R, CH), BF16),
            pltpu.VMEM((micro, C, T, R, CH), BF16),
            pltpu.VMEM((micro, C, TOK, F), BF16),
            pltpu.VMEM((micro, C, TOK, F), BF16),
            pltpu.VMEM((micro, TOK, F), F32),
            pltpu.VMEM((micro, TOK, F), F32),
            pltpu.VMEM((micro, R, 128), F32),
            pltpu.VMEM((F, CH), F32),
            pltpu.VMEM((1, D), F32),
            pltpu.VMEM((T, 1, D), F32),
            pltpu.VMEM((1, D), F32),
            pltpu.VMEM((C, 1, D), F32),
            dma((6,)),
            dma((2,)),
            dma((micro, C)),
            dma((micro, C)),
            dma((micro, C)),
            dma((micro, C)),
            dma((micro, C)),
            dma((micro, C)),
            dma((micro, C)),
            dma((micro, C)),
            dma((micro, C)),
            dma((micro, C)),
            dma((micro, C)),
            dma((micro,)),
            dma((micro,)),
            dma((micro, 4)),
            dma((micro, 4)),
            dma((2,)),
            dma((2,)),
            pltpu.SemaphoreType.REGULAR,
        ],
        cost_estimate=pl.CostEstimate(
            flops=flops, bytes_accessed=24 * D * F // 2, transcendentals=micro * TOK * F
        ),
        compiler_params=pltpu.CompilerParams(
            collective_id=0, has_side_effects=True, vmem_limit_bytes=52 * 1024 * 1024
        ),
    )(lengths, section_inputs[0], gain, cotangent, w_gate[0], w_up[0], w_down[0])
    gate, up, down, gain_out, rows = pl.pallas_call(
        writer,
        out_shape=(
            jax.ShapeDtypeStruct((CH, F), BF16),
            jax.ShapeDtypeStruct((CH, F), BF16),
            jax.ShapeDtypeStruct((F, CH), BF16),
            jax.ShapeDtypeStruct((1, D), F32),
            jax.ShapeDtypeStruct((micro, R, D), BF16),
        ),
        in_specs=[vmem] * len(outs),
        out_specs=(hbm,) * 5,
        scratch_shapes=[
            pltpu.VMEM((CH, F), BF16),
            pltpu.VMEM((CH, F), BF16),
            dma((3,)),
            dma((2, max(1, CH // 256))),
        ],
        compiler_params=pltpu.CompilerParams(vmem_limit_bytes=14 * 1024 * 1024),
    )(*outs)
    return (gate[None], up[None], down[None], gain_out, rows[None])


def solution(mesh):
    T, C = mesh.shape["tensor"], mesh.shape["dp"]
    in_specs = (
        P("section", None, ("dp", "tensor"), None),
        P("section", None),
        P("section", None, "tensor"),
        P("section", None, "tensor"),
        P("section", "tensor", None),
        P(None, ("dp", "tensor"), None),
        P(None, "dp"),
    )
    out_specs = (
        P("section", "dp", "tensor"),
        P("section", "dp", "tensor"),
        P("section", "tensor", "dp"),
        P("section", None),
        P("section", None, ("dp", "tensor"), None),
    )
    return jax.shard_map(
        functools.partial(body, T, C), mesh=mesh, in_specs=in_specs, out_specs=out_specs, check_vma=False
    )
```

```python
import functools
import math

import jax
import jax.numpy as jnp
from jax import lax
from jax.experimental import pallas as pl
from jax.experimental.pallas import tpu as pltpu
from jax.sharding import PartitionSpec as P

EPSILON = 1e-06
GELU_SCALE = math.sqrt(2.0 / math.pi)
GELU_CUBIC = 0.044715
MESH = pl.DeviceIdType.MESH
F32 = jnp.float32
BF16 = jnp.bfloat16
MICRO = 2
NN = (((1,), (0,)), ((), ()))
NT = (((1,), (1,)), ((), ()))
TN = (((0,), (0,)), ((), ()))


def dot(a, b, dims):
    return lax.dot_general(a, b, dims, preferred_element_type=F32)


def gelu_parts(pre_gate):
    tanh_arg = GELU_SCALE * (pre_gate + GELU_CUBIC * pre_gate * pre_gate * pre_gate)
    tanh_part = jnp.tanh(tanh_arg)
    gelu_value = 0.5 * pre_gate * (1.0 + tanh_part)
    gelu_slope = 0.5 * (1.0 + tanh_part) + 0.5 * pre_gate * (
        1.0 - tanh_part * tanh_part
    ) * GELU_SCALE * (1.0 + 3.0 * GELU_CUBIC * pre_gate * pre_gate)
    return (gelu_value, gelu_slope)


def kernel(
    dims,
    len_ref, x_hbm, gain_hbm, cot_hbm, wg_hbm, wu_hbm, wd_hbm,
    od_ref, ogain_ref, orow_ref, accg, nslice, pall,
    x_ref, gain_ref, cot_ref, w2, w2t, wd, wdt, nbuf, ubuf, pbuf, rbuf, obuf, nstage, relay, uslice, hgrad, hall, act, ups, inv_buf,
    accd, gsum, gten, gdp_in, gdp,
    s_w, s_d, s_n, r_n, s_u, r_u, s_p, r_p, s_o, r_hop, s_l, r_l, s_f, s_a, r_a, s_x, r_x, s_gain, r_gain, go,
):
    T, C, R, F, CH = dims
    D = C * CH
    TOK = T * R
    HALF = T // 2
    s = lax.axis_index("section")
    t = lax.axis_index("tensor")
    d = lax.axis_index("dp")

    rings = sorted(range(HALF), key=lambda q: -min(q, HALF - q))
    offsets = [(dy, dz) for dz in rings for dy in (1, 0)]
    line = t // HALF
    place = lax.rem(t, HALF)

    def tpeer(k):
        dy, dz = offsets[k - 1]
        return (1 - line if dy else line) * HALF + lax.rem(place + dz, HALF)

    def dpeer(k):
        return lax.rem(d + k, C)

    barrier = pltpu.get_barrier_semaphore()

    def greet(where):
        pl.semaphore_signal(barrier, inc=1, device_id=where, device_id_type=MESH)

    for k in range(1, T):
        greet({"tensor": tpeer(k)})
    for k in range(1, C):
        greet({"dp": dpeer(k)})
    mate = s + 1 - 2 * lax.rem(s, 2)
    for k in range(T):
        greet({"section": mate, "tensor": lax.rem(t + k, T)})

    @pl.when(s == 1)
    def _():
        greet({"section": 2})

    @pl.when(s == 2)
    def _():
        greet({"section": 1})

    cross = lax.rem(s + 2, 4)
    facing = lax.rem(t + HALF, T)
    odd = lax.rem(s, 2) == 1

    @pl.when(odd)
    def _():
        greet({"section": cross, "tensor": facing})

    @pl.when(jnp.logical_not(odd))
    def _():
        for k in range(T):
            greet({"section": cross, "tensor": lax.rem(t + k, T)})

    middle = jnp.where((s == 1) | (s == 2), 1, 0)

    def send(src, dst, ssem, rsem, where):
        pltpu.make_async_remote_copy(
            src_ref=src, dst_ref=dst, send_sem=ssem, recv_sem=rsem,
            device_id=where, device_id_type=MESH,
        ).start()

    def wait_for(ref, sem):
        pltpu.make_async_copy(ref, ref, sem).wait()

    def spread(buf, m, c, ssem, rsem):
        for k in range(1, T):
            send(buf.at[m, c, t], buf.at[m, c, t], ssem.at[m, c], rsem.at[m, c], {"tensor": tpeer(k)})

    def others(buf, m, c):
        return buf.at[m, c, pl.ds(0, T - 1)]

    inputs = [
        pltpu.make_async_copy(x_hbm, x_ref, s_w.at[3]),
        pltpu.make_async_copy(gain_hbm, gain_ref, s_w.at[4]),
        pltpu.make_async_copy(cot_hbm, cot_ref, s_w.at[5]),
    ]
    for load in inputs:
        load.start()
    loads = [
        pltpu.make_async_copy(wg_hbm, w2.at[:, pl.ds(0, F)], s_w.at[0]),
        pltpu.make_async_copy(wu_hbm, w2.at[:, pl.ds(F, F)], s_w.at[1]),
    ]
    for load in loads:
        load.start()
    lead = max(128, CH // 4)
    for n in range(2):
        pltpu.make_async_copy(wd_hbm.at[:, pl.ds(n * lead, lead)], wd.at[n], s_d.at[n]).start()

    for load in inputs:
        load.wait()

    keep_pos = lax.broadcasted_iota(jnp.int32, (R, 1), 0)
    for m in range(MICRO):
        square = jnp.zeros((R, 1), F32)
        for c in range(C):
            part = x_ref[m, :, c * CH : (c + 1) * CH].astype(F32)
            square += jnp.sum(part * part, axis=-1, keepdims=True)
        inv = lax.rsqrt(square * (1.0 / D) + EPSILON)
        inv_buf[m] = jnp.broadcast_to(inv, (R, 128))
        for c in range(C):
            cols = slice(c * CH, (c + 1) * CH)
            rows = (x_ref[m, :, cols].astype(F32) * inv * gain_ref[:, cols]).astype(BF16)
            nstage[m, c] = rows

            @pl.when(s != 2)
            def _():
                nbuf[m, c, t] = rows

    def seeds(m, c):
        keep = (keep_pos < len_ref[m, t]).astype(F32)
        return (cot_ref[m, :, c * CH : (c + 1) * CH].astype(F32) * keep).astype(BF16)

    row = (t // HALF) * HALF

    def rowpeer(k):
        return row + lax.rem(t - row + k, HALF)

    def spread_row(buf, m, c, ssem, rsem):
        for k in range(1, HALF):
            send(buf.at[m, c, t], buf.at[m, c, t], ssem.at[m, c], rsem.at[m, c], {"tensor": rowpeer(k)})

    def send_seeds(m):
        for c in range(C):
            spread_row(ubuf, m, c, s_u, r_u)

    @pl.when(s == 3)
    def _():
        for m in range(MICRO):
            for c in range(C):
                ubuf[m, c, t] = seeds(m, c)

    @pl.when(s == 1)
    def _():
        for m in range(MICRO):
            for c in range(C):
                relay[m, c, t] = seeds(m, c)

    pl.semaphore_wait(barrier, (T - 1) + (C - 1) + T + middle + jnp.where(odd, 1, T))
    def spread_n():
        for m in range(MICRO):
            for c in range(C):
                spread(nbuf, m, c, s_n, r_n)

    def slices_over_dp():
        for m in range(MICRO):
            for k in range(1, C):
                j = dpeer(k)
                send(nstage.at[m, j], nslice.at[m, d, t], s_a.at[m], r_a.at[m], {"dp": j})

    def slices_over_tensor():
        for m in range(MICRO):
            wait_for(nslice.at[m, pl.ds(0, C - 1), 0], r_a.at[m])
            for q in range(1, C):
                owner = dpeer(q)
                for k in range(1, T):
                    send(nslice.at[m, owner, t], nslice.at[m, owner, t], s_x.at[m, 0], r_x.at[m, 0],
                         {"tensor": tpeer(k)})

    @pl.when(s == 3)
    def _():
        for c in range(C):
            spread(nbuf, 0, c, s_n, r_n)
        send_seeds(0)

    @pl.when(s == 1)
    def _():
        part = pl.ds(row, HALF)
        slices_over_dp()
        for m in range(MICRO):
            for c in range(C):
                spread_row(relay, m, c, s_l, r_l)
        for m in range(MICRO):
            for c in range(C):
                wait_for(relay.at[m, c, pl.ds(0, HALF - 1)], r_l.at[m, c])
                send(relay.at[m, c, part], ubuf.at[m, c, part], s_f.at[m, c], r_u.at[m, c],
                     {"section": cross, "tensor": facing})
        spread_n()
        slices_over_tensor()
        for m in range(MICRO):
            for c in range(C):
                wait_for(relay.at[m, c, pl.ds(0, HALF)], s_f.at[m, c])
        pl.semaphore_signal(go, inc=1, device_id={"section": mate}, device_id_type=MESH)

    @pl.when(s == 2)
    def _():
        for m in range(MICRO):
            for c in range(C):
                for k in range(T):
                    send(nstage.at[m, c], relay.at[m, c, t], s_l.at[m, c], r_l.at[m, c],
                         {"section": cross, "tensor": lax.rem(t + k, T)})

    @pl.when(s == 0)
    def _():
        slices_over_dp()
        for c in range(C):
            wait_for(relay.at[0, c], r_l.at[0, c])
        spread_n()
        slices_over_tensor()
        pl.semaphore_wait(go, 1)
        for m in range(MICRO):
            for c in range(C):
                if m > 0:
                    wait_for(relay.at[m, c], r_l.at[m, c])
                send(relay.at[m, c], nbuf.at[m, c], s_f.at[m, c], r_n.at[m, c],
                     {"section": cross, "tensor": facing})

    half = max(128, CH // 4)
    pieces = D // half

    def down_load(n):
        return pltpu.make_async_copy(wd_hbm.at[:, pl.ds(n * half, half)], wd.at[n % 2], s_d.at[n % 2])

    for n in range(pieces):
        down_load(n).wait()
        wdt[n * half : (n + 1) * half, :] = wd[n % 2].T
        if n + 2 < pieces:
            down_load(n + 2).start()
    for load in loads:
        load.wait()

    def exchange_slices(buf, slices, which, m):
        for k in range(1, C):
            j = dpeer(k)
            send(buf.at[m, j], slices.at[m, d], s_x.at[m, which], r_x.at[m, which], {"dp": j})
        slices[m, d] = buf[m, d]

    def exchange_all(buf, which, m):
        for k in range(1, C):
            send(buf.at[m, d], buf.at[m, d], s_x.at[m, which], r_x.at[m, which], {"dp": dpeer(k)})

    def rows_of(buf, m, c):
        return buf[m, c].reshape(TOK, CH)

    def forward(m):
        total = jnp.zeros((TOK, 2 * F), F32)
        for c in range(C):
            @pl.when(s == 2)
            def _():
                wait_for(nbuf.at[m, c], r_n.at[m, c])

            @pl.when(s != 2)
            def _():
                wait_for(others(nbuf, m, c), r_n.at[m, c])
            if m == 0:
                @pl.when(s == 3)
                def _():
                    spread(nbuf, 1, c, s_n, r_n)
            total += dot(rows_of(nbuf, m, c), w2[c * CH : (c + 1) * CH, :], NN)
            if m == 0:
                for n in range(CH // half):
                    part = slice(c * CH + n * half, c * CH + (n + 1) * half)
                    w2t[:, part] = w2[part, :].T
        pall[m, d] = total.astype(BF16)
        exchange_all(pall, 2, m)
        pre_up = total[:, F:]
        value, slope = gelu_parts(total[:, :F])
        act[m] = value
        ups[m] = pre_up * slope

        @pl.when(s >= 2)
        def _():
            exchange_slices(nbuf, nslice, 0, m)

        @pl.when(s < 2)
        def _():
            nslice[m, d] = nbuf[m, d]

    def expand(m):
        wait_for(pall.at[m, pl.ds(0, C - 1)], r_x.at[m, 2])
        wait_for(pall.at[m, pl.ds(0, C - 1)], s_x.at[m, 2])

        def one(j, carry):
            pre_gate = pall[m, j, :, :F].astype(F32)
            pre_up = pall[m, j, :, F:].astype(F32)
            value, slope = gelu_parts(pre_gate)
            hall[m, j] = (value * pre_up).astype(BF16)
            pall[m, j, :, :F] = (pre_up * slope).astype(BF16)
            pall[m, j, :, F:] = value.astype(BF16)
            return carry

        lax.fori_loop(0, C, one, 0)

    def expand_grads(m):
        def one(j, carry):
            upstream = hgrad[m, j]
            pall[m, j, :, :F] = upstream * pall[m, j, :, :F]
            pall[m, j, :, F:] = upstream * pall[m, j, :, F:]
            return carry

        lax.fori_loop(0, C, one, 0)

    def products(m):
        grad_hidden = jnp.zeros((TOK, F), F32)
        for c in range(C):
            @pl.when(odd)
            def _():
                wait_for(others(ubuf, m, c), r_u.at[m, c])

            @pl.when(jnp.logical_not(odd))
            def _():
                wait_for(ubuf.at[m, c], r_u.at[m, c])
            if m == 0:
                @pl.when(s == 3)
                def _():
                    spread_row(ubuf, 1, c, s_u, r_u)
            grad_hidden += dot(rows_of(ubuf, m, c), wdt[c * CH : (c + 1) * CH, :], NN)
        hgrad[m, d] = grad_hidden.astype(BF16)
        both = jnp.concatenate(
            [(grad_hidden * ups[m]).astype(BF16), (grad_hidden * act[m]).astype(BF16)], axis=1
        )
        for c in range(C):
            term = dot(both, w2t[:, c * CH : (c + 1) * CH], NN).astype(BF16)
            pbuf[m, c] = term.reshape(T, R, CH)
            rbuf[m, c, t] = pbuf[m, c, t]
            for k in range(1, T):
                j = tpeer(k)
                send(pbuf.at[m, c, j], rbuf.at[m, c, t], s_p.at[m, c], r_p.at[m, c], {"tensor": j})
            if c == 0:
                exchange_slices(ubuf, uslice, 1, m)
                exchange_all(hgrad, 3, m)
    def send_gain():
        for k in range(1, T):
            send(gsum, gten.at[t], s_gain.at[0], r_gain.at[0], {"tensor": tpeer(k)})

    def finish(m):
        inv = inv_buf[m, :, 0:1]
        mean = jnp.zeros((R, 1), F32)
        sums = []
        for c in range(C):
            cols = slice(c * CH, (c + 1) * CH)
            wait_for(others(rbuf, m, c), r_p.at[m, c])
            grad_normed = jnp.zeros((R, CH), F32)
            for j in range(T):
                grad_normed += rbuf[m, c, j].astype(F32)
            part = x_ref[m, :, cols].astype(F32)
            scaled = grad_normed * gain_ref[:, cols]
            mean += jnp.sum(scaled * part, axis=-1, keepdims=True)
            gain_part = jnp.sum(grad_normed * part * inv, axis=0, keepdims=True)
            if m == 0:
                gsum[:, cols] = gain_part
            else:
                gsum[:, cols] += gain_part
            sums.append(scaled)
        if m == MICRO - 1:
            pl.when(s == 0)(send_gain)
        factor = inv * inv * inv * (mean * (1.0 / D))
        for c in range(C):
            cols = slice(c * CH, (c + 1) * CH)
            part = x_ref[m, :, cols].astype(F32)
            result = ubuf[m, c, t].astype(F32) + inv * sums[c] - part * factor
            rows = result.astype(BF16)
            obuf[m, c] = rows
            orow_ref[m, :, cols] = rows

            @pl.when(odd)
            def _():
                for k in range(1, T + 1):
                    send(obuf.at[m, c], ubuf.at[m, c, t], s_o.at[m, c], r_u.at[m, c],
                         {"section": s - 1, "tensor": tpeer(k)})

            @pl.when(s == 2)
            def _():
                send(obuf.at[m, c], ubuf.at[m, c, t], s_o.at[m, c], r_hop.at[m, c], {"section": s - 1})

    forward(0)
    pl.when(s < 2)(lambda: forward(1))

    @pl.when(s == 1)
    def _():
        for m in range(MICRO):
            for c in range(C):
                wait_for(ubuf.at[m, c, t], r_hop.at[m, c])
                spread(ubuf, m, c, s_u, r_u)

    @pl.when(s == 0)
    def _():
        for m in range(MICRO):
            expand(m)

    products(0)
    pl.when(s >= 2)(lambda: forward(1))
    products(1)

    finish(0)

    count = C * TOK
    step = min(256, CH)

    def slices_arrived(m):
        @pl.when(s >= 2)
        def _():
            wait_for(nslice.at[m, pl.ds(0, C - 1)], r_x.at[m, 0])

        @pl.when(s < 2)
        def _():
            wait_for(nslice.at[m, pl.ds(0, C - 1), pl.ds(0, T - 1)], r_x.at[m, 0])

        wait_for(uslice.at[m, pl.ds(0, C - 1)], r_x.at[m, 1])

    def grads_arrived(m):
        wait_for(hgrad.at[m, pl.ds(0, C - 1)], r_x.at[m, 3])
        expand_grads(m)

    def term_down(m, cols):
        return dot(hall[m].reshape(count, F), uslice[m, :, :, :, cols].reshape(count, step), TN)

    def first_terms():
        slices_arrived(0)
        for n in range(CH // step):
            cols = slice(n * step, (n + 1) * step)
            accd[:, cols] = term_down(0, cols)
        grads_arrived(0)
        for n in range(CH // step):
            part = slice(n * step, (n + 1) * step)
            accg[part, :] = gate_up_term(nslice, pall, 0, part)

    pl.when(s == 0)(first_terms)
    finish(1)

    gten[t] = gsum[...]
    pl.when(s > 0)(send_gain)

    @pl.when(s > 0)
    def _():
        for m in range(MICRO):
            expand(m)

    pl.when(s > 0)(first_terms)
    slices_arrived(1)
    for n in range(CH // step):
        cols = slice(n * step, (n + 1) * step)
        od_ref[:, cols] = (accd[:, cols] + term_down(1, cols)).astype(BF16)

    wait_for(gten.at[pl.ds(0, T - 1)], r_gain.at[0])
    gain_total = gten[0]
    for j in range(1, T):
        gain_total += gten[j]
    gdp_in[...] = gain_total
    gdp[d] = gain_total
    for k in range(1, C):
        send(gdp_in, gdp.at[d], s_gain.at[1], r_gain.at[1], {"dp": dpeer(k)})

    grads_arrived(1)

    for m in range(MICRO):
        for c in range(C):
            wait_for(others(pbuf, m, c), s_p.at[m, c])

            @pl.when(odd)
            def _():
                wait_for(ubuf.at[m, c], s_o.at[m, c])

            @pl.when(s == 0)
            def _():
                wait_for(relay.at[m, c], s_f.at[m, c])

            @pl.when(s == 1)
            def _():
                wait_for(relay.at[m, c, pl.ds(0, HALF - 1)], s_l.at[m, c])
                wait_for(others(ubuf, m, c), s_u.at[m, c])

            @pl.when(s == 3)
            def _():
                wait_for(ubuf.at[m, c, pl.ds(0, HALF - 1)], s_u.at[m, c])

            @pl.when(s != 2)
            def _():
                wait_for(others(nbuf, m, c), s_n.at[m, c])

            @pl.when(s == 2)
            def _():
                wait_for(relay.at[m, c], s_l.at[m, c])
                wait_for(obuf.at[m, c], s_o.at[m, c])
        @pl.when(s >= 2)
        def _():
            wait_for(nslice.at[m, pl.ds(0, C - 1)], s_x.at[m, 0])

        @pl.when(s < 2)
        def _():
            wait_for(nslice.at[m, pl.ds(0, C - 1), 0], s_a.at[m])
            wait_for(nslice.at[m, pl.ds(0, C - 1), pl.ds(0, T - 1)], s_x.at[m, 0])

        wait_for(uslice.at[m, pl.ds(0, C - 1)], s_x.at[m, 1])
        wait_for(hgrad.at[m, pl.ds(0, C - 1)], s_x.at[m, 3])
    wait_for(gdp.at[pl.ds(0, C - 1)], r_gain.at[1])
    gain_total = gdp[0]
    for j in range(1, C):
        gain_total += gdp[j]
    ogain_ref[...] = gain_total
    wait_for(gten.at[pl.ds(0, T - 1)], s_gain.at[0])
    wait_for(gdp.at[pl.ds(0, C - 1)], s_gain.at[1])


def gate_up_term(nslice, gall, m, rows):
    C, T, R, _ = nslice.shape[1:]
    step = rows.stop - rows.start
    left = nslice[m, :, :, :, rows].reshape(C * T * R, step)
    return dot(left, gall[m].reshape(C * T * R, gall.shape[-1]), TN)


def writer(down, gain, rows, accg, nslice, gall, og, ou, od, ogain, orow, vg, vu, sems, tile_sems):
    copies = [
        pltpu.make_async_copy(down, od, sems.at[0]),
        pltpu.make_async_copy(gain, ogain, sems.at[1]),
        pltpu.make_async_copy(rows, orow, sems.at[2]),
    ]
    for copy in copies:
        copy.start()
    CH, F = vg.shape
    step = min(256, CH)
    for n in range(CH // step):
        part = slice(n * step, (n + 1) * step)
        total = accg[part, :] + gate_up_term(nslice, gall, MICRO - 1, part)
        vg[part, :] = total[:, :F].astype(BF16)
        vu[part, :] = total[:, F:].astype(BF16)
        for which, (src, dst) in enumerate(((vg, og), (vu, ou))):
            block = pl.ds(n * step, step)
            copy = pltpu.make_async_copy(src.at[block], dst.at[block], tile_sems.at[which, n])
            copy.start()
            copies.append(copy)
    for copy in copies:
        copy.wait()


def body(T, C, section_inputs, gain, w_gate, w_up, w_down, cotangent, lengths):
    _, micro, R, D = section_inputs.shape
    F = w_gate.shape[2]
    CH = D // C
    TOK = T * R
    dims = (T, C, R, F, CH)
    vmem = pl.BlockSpec(memory_space=pltpu.VMEM)
    smem = pl.BlockSpec(memory_space=pltpu.SMEM)
    hbm = pl.BlockSpec(memory_space=pl.ANY)
    dma = pltpu.SemaphoreType.DMA
    flops = 2 * micro * 8 * TOK * D * F
    outs = pl.pallas_call(
        functools.partial(kernel, dims),
        out_shape=(
            pltpu.VMEM((F, CH), BF16),
            pltpu.VMEM((1, D), F32),
            pltpu.VMEM((micro, R, D), BF16),
            pltpu.VMEM((CH, 2 * F), F32),
            pltpu.VMEM((micro, C, T, R, CH), BF16),
            pltpu.VMEM((micro, C, TOK, 2 * F), BF16),
        ),
        in_specs=[smem] + [hbm] * 6,
        out_specs=(vmem,) * 6,
        scratch_shapes=[
            pltpu.VMEM((micro, R, D), BF16),
            pltpu.VMEM((1, D), F32),
            pltpu.VMEM((micro, R, D), BF16),
            pltpu.VMEM((D, 2 * F), BF16),
            pltpu.VMEM((2 * F, D), BF16),
            pltpu.VMEM((2, F, max(128, CH // 4)), BF16),
            pltpu.VMEM((D, F), BF16),
            pltpu.VMEM((micro, C, T, R, CH), BF16),
            pltpu.VMEM((micro, C, T, R, CH), BF16),
            pltpu.VMEM((micro, C, T, R, CH), BF16),
            pltpu.VMEM((micro, C, T, R, CH), BF16),
            pltpu.VMEM((micro, C, R, CH), BF16),
            pltpu.VMEM((micro, C, R, CH), BF16),
            pltpu.VMEM((micro, C, T, R, CH), BF16),
            pltpu.VMEM((micro, C, T, R, CH), BF16),
            pltpu.VMEM((micro, C, TOK, F), BF16),
            pltpu.VMEM((micro, C, TOK, F), BF16),
            pltpu.VMEM((micro, TOK, F), F32),
            pltpu.VMEM((micro, TOK, F), F32),
            pltpu.VMEM((micro, R, 128), F32),
            pltpu.VMEM((F, CH), F32),
            pltpu.VMEM((1, D), F32),
            pltpu.VMEM((T, 1, D), F32),
            pltpu.VMEM((1, D), F32),
            pltpu.VMEM((C, 1, D), F32),
            dma((6,)),
            dma((2,)),
            dma((micro, C)),
            dma((micro, C)),
            dma((micro, C)),
            dma((micro, C)),
            dma((micro, C)),
            dma((micro, C)),
            dma((micro, C)),
            dma((micro, C)),
            dma((micro, C)),
            dma((micro, C)),
            dma((micro, C)),
            dma((micro,)),
            dma((micro,)),
            dma((micro, 4)),
            dma((micro, 4)),
            dma((2,)),
            dma((2,)),
            pltpu.SemaphoreType.REGULAR,
        ],
        cost_estimate=pl.CostEstimate(
            flops=flops, bytes_accessed=24 * D * F // 2, transcendentals=micro * TOK * F
        ),
        compiler_params=pltpu.CompilerParams(
            collective_id=0, has_side_effects=True, vmem_limit_bytes=52 * 1024 * 1024
        ),
    )(lengths, section_inputs[0], gain, cotangent, w_gate[0], w_up[0], w_down[0])
    gate, up, down, gain_out, rows = pl.pallas_call(
        writer,
        out_shape=(
            jax.ShapeDtypeStruct((CH, F), BF16),
            jax.ShapeDtypeStruct((CH, F), BF16),
            jax.ShapeDtypeStruct((F, CH), BF16),
            jax.ShapeDtypeStruct((1, D), F32),
            jax.ShapeDtypeStruct((micro, R, D), BF16),
        ),
        in_specs=[vmem] * len(outs),
        out_specs=(hbm,) * 5,
        scratch_shapes=[
            pltpu.VMEM((CH, F), BF16),
            pltpu.VMEM((CH, F), BF16),
            dma((3,)),
            dma((2, max(1, CH // 256))),
        ],
        compiler_params=pltpu.CompilerParams(vmem_limit_bytes=14 * 1024 * 1024),
    )(*outs)
    return (gate[None], up[None], down[None], gain_out, rows[None])


def solution(mesh):
    T, C = mesh.shape["tensor"], mesh.shape["dp"]
    in_specs = (
        P("section", None, ("dp", "tensor"), None),
        P("section", None),
        P("section", None, "tensor"),
        P("section", None, "tensor"),
        P("section", "tensor", None),
        P(None, ("dp", "tensor"), None),
        P(None, "dp"),
    )
    out_specs = (
        P("section", "dp", "tensor"),
        P("section", "dp", "tensor"),
        P("section", "tensor", "dp"),
        P("section", None),
        P("section", None, ("dp", "tensor"), None),
    )
    return jax.shard_map(
        functools.partial(body, T, C), mesh=mesh, in_specs=in_specs, out_specs=out_specs, check_vma=False
    )
```
